32 devices in a mesh: seq: 4 (over y, core), exp: 8 (over z, x).
Axes of the slice: x: 2, y: 2, z: 4, core: 2. Of those that a mesh axis runs over, the one named last changes fastest.
Arguments:
- tokens: bfloat16 [8, 2048, 1280], P('exp', 'seq'), may hold values from -64 to 64
- router: bfloat16 [1280, 16], replicated, may hold values from -2 to 2
- w_in: bfloat16 [8, 1280, 5120], P('exp', None, 'seq'), may hold values from -0.15625 to 0.15625
- w_out: bfloat16 [8, 5120, 1280], P('exp', 'seq'), may hold values from -0.078125 to 0.078125
- grad_out: bfloat16 [8, 2048, 1280], P('exp', 'seq'), may hold values from -6 to 6
Outputs:
- mixed: bfloat16 [8, 2048, 1280], P('exp', 'seq')
- d_tokens: bfloat16 [8, 2048, 1280], P('exp', 'seq')
- d_router: float32 [1280, 16], P(('seq', 'exp'))
- d_w_in: bfloat16 [8, 1280, 5120], P('exp', None, 'seq')
- d_w_out: bfloat16 [8, 5120, 1280], P('exp', 'seq')
The draws below stay inside these ranges and needn't reach their ends.
All inputs are finite; a program needn't handle non-finite values.
Results may differ from the reference program's by a relative error of at most 0.034.
Values may be sent and summed in bfloat16 or wider, within the bound.
No kernel may reach another device: no remote copies, remote signals or barrier semaphores. Data moves between devices by JAX's collectives and lax.ppermute only.
A program may use at most 64 MiB of HBM per device.

```python
import math
import jax
import jax.numpy as jnp
from jax import lax

MODEL_WIDTH = 1280
FF = 5120
SLOTS_PER_EXPERT = 2
EXPERT_COUNT = 8
TOTAL_SLOTS = 16
CLIP_COUNT = 8
LEN = 2048


def shared_normal(key):
    return jnp.clip(jax.random.normal(key, (MODEL_WIDTH, TOTAL_SLOTS), jnp.float32), -4.0, 4.0)


def draw_router(key, part):
    base = shared_normal(key)
    return (2.5 * base / math.sqrt(MODEL_WIDTH)).astype(jnp.bfloat16)


def draw_tokens(key, part):
    key = jax.random.fold_in(key, 7)
    split_random_keys = jax.random.split(key, 1)
    noise = jnp.clip(jax.random.normal(split_random_keys[0], (CLIP_COUNT, LEN, MODEL_WIDTH), jnp.float32), -6.0, 6.0)
    return noise.astype(jnp.bfloat16)


def levels(key, extent, cuts, low, high):
    loudness = 1.0
    for axis_at, parts in cuts:
        steps = jax.random.uniform(jax.random.fold_in(jax.random.fold_in(key, 6), axis_at), (parts,), jnp.float32, low / len(cuts), high / len(cuts))
        loudness = loudness * jnp.repeat(jnp.exp(steps), extent[axis_at] // parts).reshape((-1,) + (1,) * (len(extent) - 1 - axis_at))
    return loudness


def bell_draw(rng, dims, scale, most, cuts=(), kind=jnp.bfloat16):
    array = jax.random.normal(rng, dims, jnp.float32) * scale
    if len(cuts) > 0:
        array = levels(rng, dims, cuts, -0.22, 0.18) * array
    return jnp.clip(array, min=-most, max=most).astype(kind)


def setup_inputs(seed: int = 0) -> dict:
    splits = jax.random.split(jax.random.key(seed), 6)
    tokens = draw_tokens(jax.random.fold_in(splits[5], 71), 0)
    router = draw_router(jax.random.fold_in(splits[5], 71), 0)
    w_in = bell_draw(splits[2], (EXPERT_COUNT, MODEL_WIDTH, FF), MODEL_WIDTH ** -0.5, 0.15625, ((0, 8), (2, 4)))
    w_out = bell_draw(splits[3], (EXPERT_COUNT, FF, MODEL_WIDTH), FF ** -0.5, 0.078125, ((0, 8), (1, 4)))
    grad_out = bell_draw(splits[4], (CLIP_COUNT, LEN, MODEL_WIDTH), 1.0, 6.0, ((0, 8), (1, 4)))
    return {"tokens": tokens, "router": router, "w_in": w_in, "w_out": w_out, "grad_out": grad_out}


def gelu_grad(values):
    return 0.5 * (1.0 + lax.erf(values * (1.0 / math.sqrt(2.0)))) + values * jnp.exp(-0.5 * values * values) / math.sqrt(2.0 * math.pi)

def reference(tokens, router, w_in, w_out, grad_out):
    feats = tokens.astype(jnp.float32)
    phi = router.astype(jnp.float32)
    logits = jnp.einsum('ctd,dj->cjt', feats, phi)
    col_top = lax.optimization_barrier(jnp.max(logits, axis=2, keepdims=True))
    col_exp = jnp.exp(logits - col_top)
    dispatch = col_exp / lax.optimization_barrier(jnp.sum(col_exp, axis=2, keepdims=True))
    dispatch_b = dispatch.astype(jnp.bfloat16)
    slots_in = jnp.einsum('cjt,ctd->cjd', dispatch_b.astype(jnp.float32), feats).astype(jnp.bfloat16)
    rows = slots_in.reshape(CLIP_COUNT, EXPERT_COUNT, SLOTS_PER_EXPERT, MODEL_WIDTH).transpose(1, 0, 2, 3).reshape(EXPERT_COUNT, CLIP_COUNT * SLOTS_PER_EXPERT, MODEL_WIDTH)
    hidden = jnp.einsum('erd,edf->erf', rows.astype(jnp.float32), w_in.astype(jnp.float32))
    activated = jax.nn.gelu(hidden, approximate=False).astype(jnp.bfloat16)
    rows_per_expert = jnp.einsum('erf,efd->erd', activated.astype(jnp.float32), w_out.astype(jnp.float32)).astype(jnp.bfloat16)
    slot_output = rows_per_expert.reshape(EXPERT_COUNT, CLIP_COUNT, SLOTS_PER_EXPERT, MODEL_WIDTH).transpose(1, 0, 2, 3).reshape(CLIP_COUNT, TOTAL_SLOTS, MODEL_WIDTH)
    row_top = lax.optimization_barrier(jnp.max(logits, axis=1, keepdims=True))
    row_exp = jnp.exp(logits - row_top)
    combine = row_exp / lax.optimization_barrier(jnp.sum(row_exp, axis=1, keepdims=True))
    combine_b = combine.astype(jnp.bfloat16)
    slots_f = slot_output.astype(jnp.float32)
    mixed = jnp.einsum('cjt,cjd->ctd', combine_b.astype(jnp.float32), slots_f).astype(jnp.bfloat16)
    cotangent = grad_out.astype(jnp.float32)
    d_slots_out = jnp.einsum('cjt,ctd->cjd', combine_b.astype(jnp.float32), cotangent).astype(jnp.bfloat16)
    d_combine = jnp.einsum('cjd,ctd->cjt', slots_f, cotangent)
    d_logit_c = combine * (d_combine - lax.optimization_barrier(jnp.sum(combine * d_combine, axis=1, keepdims=True)))
    d_rows = d_slots_out.reshape(CLIP_COUNT, EXPERT_COUNT, SLOTS_PER_EXPERT, MODEL_WIDTH).transpose(1, 0, 2, 3).reshape(EXPERT_COUNT, CLIP_COUNT * SLOTS_PER_EXPERT, MODEL_WIDTH)
    d_rows_f = d_rows.astype(jnp.float32)
    d_activated = jnp.einsum('erd,efd->erf', d_rows_f, w_out.astype(jnp.float32))
    d_hidden = (d_activated * gelu_grad(hidden)).astype(jnp.bfloat16)
    d_w_out = jnp.einsum('erf,erd->efd', activated.astype(jnp.float32), d_rows_f).astype(jnp.bfloat16)
    d_w_in = jnp.einsum('erd,erf->edf', rows.astype(jnp.float32), d_hidden.astype(jnp.float32)).astype(jnp.bfloat16)
    input_rows_gradient = jnp.einsum('erf,edf->erd', d_hidden.astype(jnp.float32), w_in.astype(jnp.float32)).astype(jnp.bfloat16)
    slot_input_gradient = input_rows_gradient.reshape(EXPERT_COUNT, CLIP_COUNT, SLOTS_PER_EXPERT, MODEL_WIDTH).transpose(1, 0, 2, 3).reshape(CLIP_COUNT, TOTAL_SLOTS, MODEL_WIDTH)
    d_slots_f = slot_input_gradient.astype(jnp.float32)
    d_dispatch = jnp.einsum('cjd,ctd->cjt', d_slots_f, feats)
    d_logit_d = dispatch * (d_dispatch - lax.optimization_barrier(jnp.sum(dispatch * d_dispatch, axis=2, keepdims=True)))
    d_logit_b = (d_logit_c + d_logit_d).astype(jnp.bfloat16)
    d_logit_f = d_logit_b.astype(jnp.float32)
    d_tokens = (jnp.einsum('cjt,cjd->ctd', dispatch_b.astype(jnp.float32), d_slots_f) + jnp.einsum('cjt,dj->ctd', d_logit_f, phi)).astype(jnp.bfloat16)
    d_router = jnp.einsum('ctd,cjt->dj', feats, d_logit_f)
    return (mixed, d_tokens, d_router, d_w_in, d_w_out)
```

```python
import functools
import math

import jax
import jax.numpy as jnp
from jax import lax
from jax.experimental import pallas as pl
from jax.experimental.pallas import tpu as pltpu
from jax.sharding import PartitionSpec as P

F32 = jnp.float32
BF16 = jnp.bfloat16
LANES = 128
FIRST_FLOPS = 1 << 40
PACK_MIB = 8
EXPERT_MIB = 24
PACK_FLOPS = 1 << 36
OUTER_FLOPS = 1 << 36
VMEM = pl.BlockSpec(memory_space=pltpu.VMEM)
HBM = pl.BlockSpec(memory_space=pltpu.HBM)


def dot(a, b, ca, cb):
    return lax.dot_general(a, b, (((ca,), (cb,)), ((), ())), preferred_element_type=F32)


def pieces(x):
    hi = x.astype(BF16)
    rest = x - hi.astype(F32)
    mid = rest.astype(BF16)
    return hi, mid, (rest - mid.astype(F32)).astype(BF16)


ERFC = (
    0.17087277, -0.82215223, 1.48851587, -1.13520398, 0.27886807,
    -0.18628806, 0.09678418, 0.37409196, 1.00002368, -1.26551223,
)


def gelu_parts(h):
    z = jnp.abs(h) * math.sqrt(0.5)
    t = 1.0 / (1.0 + 0.5 * z)
    poly = jnp.full_like(t, ERFC[0])
    for coefficient in ERFC[1:]:
        poly = poly * t + coefficient
    tail = 0.5 * t * jnp.exp(poly - z * z)
    cdf = jnp.where(h < 0, tail, 1.0 - tail)
    pdf = jnp.exp(-0.5 * h * h) * (1.0 / math.sqrt(2.0 * math.pi))
    return h * cdf, cdf + h * pdf


def call(body, out, vmem_mib, flops, nbytes, scratch=(), in_hbm=(), out_hbm=()):
    def run(*args):
        specs = [HBM if n in in_hbm else VMEM for n in range(len(args))]
        return pl.pallas_call(
            body,
            out_shape=tuple(jax.ShapeDtypeStruct(s, d) for s, d in out),
            in_specs=specs,
            out_specs=tuple(HBM if n in out_hbm else VMEM for n in range(len(out))),
            scratch_shapes=list(scratch),
            compiler_params=pltpu.CompilerParams(vmem_limit_bytes=int(vmem_mib * 2**20)),
            cost_estimate=pl.CostEstimate(flops=flops, bytes_accessed=nbytes, transcendentals=0),
        )(*args)

    return run


def shards(ns, ne, tokens, router, w_in, w_out, grad_out):
    feats, cotangent, w1, w2 = tokens[0], grad_out[0], w_in[0], w_out[0]
    length, width = feats.shape
    slots = router.shape[1]
    per = slots // ne
    hidden_part = w1.shape[1]
    half = width // 2
    wide = width + LANES
    cut = width // (ns * ne)

    def to_seq(x, k):
        return lax.ppermute(x, "seq", [(i, i ^ k) for i in range(ns)])

    def to_all(x):
        return lax.all_to_all(x, ("seq", "exp"), 0, 0, tiled=True)

    def pairs_of(a, b, n):
        at = slice(n * per, (n + 1) * per)
        return jnp.concatenate([a[at], b[at]], axis=0).astype(BF16)

    def stat_tile(*columns):
        lane = lax.broadcasted_iota(jnp.int32, (slots, LANES), 1)
        tile = jnp.zeros((slots, LANES), F32)
        for n, v in enumerate(columns):
            tile = jnp.where(lane == n, v.astype(F32), tile)
        return tile

    def first_kernel(out_ref):
        out_ref[...] = jnp.zeros((8, LANES), F32)

    (begun,) = call(first_kernel, [((8, LANES), F32)], 8, FIRST_FLOPS, 0)()

    def start_kernel(x_ref, r_ref, g_ref, _, part_ref, keep_ref, half_ref):
        x = x_ref[...]
        logits = dot(r_ref[...], x, 1, 1)
        top = jnp.max(logits, axis=1, keepdims=True)
        p = jnp.exp(logits - top)
        p_b = p.astype(BF16)
        total = jnp.sum(p, axis=1, keepdims=True)
        total_b = jnp.sum(p_b.astype(F32), axis=1, keepdims=True)
        e = jnp.exp(logits - jnp.max(logits, axis=0, keepdims=True))
        combine_b = (e / jnp.sum(e, axis=0, keepdims=True)).astype(BF16)
        a = dot(p_b, x, 1, 0)
        b = dot(combine_b, g_ref[...], 1, 0)
        part_ref[:, :width] = a
        part_ref[:, width:wide] = stat_tile(top, total, total_b)
        half_ref[0] = b[:, :half]
        half_ref[1] = b[:, half:]
        core = lax.rem(lax.axis_index("seq"), 2)
        part_ref[:, wide:] = half_ref[1 - core]
        keep_ref[...] = half_ref[core]

    part, keep = call(
        start_kernel,
        [((slots, wide + half), F32), ((slots, half), F32)],
        24,
        6 * slots * length * width,
        4 * length * width,
        [pltpu.VMEM((2, slots, half), F32)],
        in_hbm=(3,),
    )(feats, router.T, cotangent, begun)

    def merged(l_ref, r_ref):
        tops, totals, totals_b = (
            [r[:, width + n : width + n + 1] for r in (l_ref, r_ref)] for n in range(3)
        )
        top = jnp.maximum(*tops)
        scale = [jnp.exp(m - top) for m in tops]
        total, total_b = (scale[0] * v[0] + scale[1] * v[1] for v in (totals, totals_b))
        return scale[0] * l_ref[:, :width] + scale[1] * r_ref[:, :width], top, total, total_b

    def pack_kernel(l_ref, r_ref, keep_ref, part_ref, send_ref, half_ref):
        a, top, total, total_b = merged(l_ref, r_ref)
        part_ref[:, :width] = a
        part_ref[:, width:] = stat_tile(top, total, total_b)
        half_ref[0] = a[:, :half]
        half_ref[1] = a[:, half:]
        a = half_ref[lax.rem(lax.axis_index("seq"), 2)]
        b = keep_ref[...] + r_ref[:, wide:]
        a = jnp.concatenate([a, stat_tile(*pieces(top), *pieces(total_b))], axis=1)
        b = jnp.concatenate([b, jnp.zeros((slots, LANES), F32)], axis=1)
        for e in range(ne):
            chunk = pairs_of(a, b, e)
            for s in range(ns):
                send_ref[s * ne + e] = chunk

    part, send = call(
        pack_kernel,
        [((slots, wide), F32), ((ns * ne, 2 * per, half + LANES), BF16)],
        PACK_MIB,
        PACK_FLOPS,
        8 * slots * wide,
        [pltpu.VMEM((2, slots, half), F32)],
    )(part, to_seq(part, 1), keep)
    rows_in = to_all(send)

    def expert_kernel(*refs):
        w2_ref, in_ref, w1_ref, x_ref, dy_ref, act_ref, dh_ref, out_ref, keep_ref, *scratch = refs
        (half_ref,) = scratch
        tops, totals = [], []
        for s in range(0, ns, 2):
            tile = jnp.concatenate(
                [in_ref[s * ne + c, :, half:].astype(F32)[:per] for c in range(ne)], axis=0
            )
            tops.append(tile[:, 0:1] + tile[:, 1:2] + tile[:, 2:3])
            totals.append(tile[:, 3:4] + tile[:, 4:5] + tile[:, 5:6])
        top = functools.reduce(jnp.maximum, tops)
        scale = [jnp.exp(m - top) for m in tops]
        total = sum(w * v for w, v in zip(scale, totals))
        scale = [w / total for w in scale]
        xs, dys = [[], []], [[], []]
        for core in range(2):
            for c in range(ne):
                at = slice(c * per, (c + 1) * per)
                x, dy = 0.0, 0.0
                for w, s in zip(scale, range(core, ns, 2)):
                    v = in_ref[s * ne + c, :, :half].astype(F32)
                    x += w[at] * v[:per]
                    dy += v[per:]
                xs[core].append(x)
                dys[core].append(dy)
        x, dy = (
            jnp.concatenate([jnp.concatenate(v, axis=0) for v in side], axis=1).astype(BF16)
            for side in (xs, dys)
        )
        x_ref[...] = x
        dy_ref[...] = dy
        w2v = w2_ref[...]
        d_act = dot(dy, w2v, 1, 1)
        act, slope = gelu_parts(dot(x, w1_ref[...], 1, 0))
        act = act.astype(BF16)
        act_ref[...] = act
        dh = (d_act * slope).astype(BF16)
        dh_ref[...] = dh
        y = dot(act, w2v, 1, 0)
        dx = dot(dh, w1_ref[...], 1, 1)
        for core in range(2):
            at = slice(core * half, (core + 1) * half)
            half_ref[core, :slots] = y[:, at]
            half_ref[core, slots:] = dx[:, at]
        core = lax.rem(lax.axis_index("seq"), 2)
        out_ref[...] = half_ref[1 - core]
        keep_ref[...] = half_ref[core]

    x_rows, dy_rows, act, dh, out, keep = call(
        expert_kernel,
        [((slots, width), BF16)] * 2
        + [((slots, hidden_part), BF16)] * 2
        + [((2 * slots, half), F32)] * 2,
        EXPERT_MIB,
        8 * slots * width * hidden_part,
        4 * width * hidden_part,
        [
            pltpu.VMEM((2, 2 * slots, half), F32),
        ],
    )(w2, rows_in, w1)

    def pack_back_kernel(l_ref, r_ref, send_hbm, near_ref, sems):
        full = l_ref[...] + r_ref[...]
        for c in range(ne):
            near_ref[c] = pairs_of(full[:slots], full[slots:], c)
        copies = [
            pltpu.make_async_copy(near_ref, send_hbm.at[pl.ds(s * ne, ne)], sems.at[s]) for s in range(ns)
        ]
        for copy in copies:
            copy.start()
        for copy in copies:
            copy.wait()

    (send,) = call(
        pack_back_kernel,
        [((ns * ne, 2 * per, half), BF16)],
        PACK_MIB,
        2 * slots * width,
        8 * slots * width,
        [pltpu.VMEM((ne, 2 * per, half), BF16), pltpu.SemaphoreType.DMA((ns,))],
        out_hbm=(0,),
    )(keep, to_seq(out, 1))
    rows_back = to_all(send)

    def outer(steps, build, shapes, *operands):
        def body(*refs):
            ins, outs, done_ref, near, sems = refs[:-6], refs[-6:-4], refs[-4], refs[-3:-1], refs[-1]
            pairs = build(*[r[...] for r in ins])
            copies = []
            for n in range(steps):
                for m, (left, right) in enumerate(pairs):
                    step = near[m].shape[0] // steps
                    at = slice(n * step, (n + 1) * step)
                    near[m][at] = dot(left[:, at], right, 0, 0).astype(BF16)
                    copy = pltpu.make_async_copy(near[m].at[at], outs[m].at[at], sems.at[2 * n + m])
                    copy.start()
                    copies.append(copy)
            done_ref[...] = jnp.zeros((8, LANES), F32)
            for copy in copies:
                copy.wait()

        return call(
            body,
            [(shape, BF16) for shape in shapes] + [((8, LANES), F32)],
            16,
            OUTER_FLOPS,
            sum(2 * m * n for m, n in shapes),
            [pltpu.VMEM(shape, BF16) for shape in shapes] + [pltpu.SemaphoreType.DMA((2 * steps,))],
            out_hbm=(0, 1),
        )(*operands)

    d_w_out, d_w_in, written = outer(
        5,
        lambda act, dy, x, dh: ((act, dy), (x, dh)),
        ((hidden_part, width), (width, hidden_part)),
        act,
        dy_rows,
        x_rows,
        dh,
    )

    def merge_kernel(l_ref, r_ref, out_ref):
        a, *stats = merged(l_ref, r_ref)
        out_ref[:, :width] = a
        out_ref[:, width:] = stat_tile(*stats)

    bits = (ns - 1).bit_length()
    for bit in range(1, bits - 1):
        (part,) = call(
            merge_kernel, [((slots, wide), F32)], 8, 4 * slots * width, 12 * slots * width
        )(part, to_seq(part, 1 << bit))

    def softmax_kernel(_, l_ref, r_ref, route_ref, x_ref, row_ref, combine_ref, dispatch_ref):
        a, top, total, total_b = merged(l_ref, r_ref)
        row_ref[...] = a / total_b
        logits = dot(route_ref[...], x_ref[...], 1, 1)
        e = jnp.exp(logits - jnp.max(logits, axis=0, keepdims=True))
        combine_ref[...] = e / jnp.sum(e, axis=0, keepdims=True)
        dispatch_ref[...] = jnp.exp(logits - top) / total

    clip_rows, combine, dispatch = call(
        softmax_kernel,
        [((slots, width), F32), ((slots, length), F32), ((slots, length), F32)],
        8,
        2 * slots * length * width,
        2 * length * width,
        in_hbm=(0,),
    )(written, part, to_seq(part, 1 << (bits - 1)), router.T, feats)

    def logit_kernel(in_ref, a_ref, c_ref, d_ref, x_ref, g_ref, l_ref, y_ref, dx_ref, out):
        y, dx = [], []
        for core in range(2):
            got = [sum(in_ref[s * ne + e].astype(F32) for s in range(core, ns, 2)) for e in range(ne)]
            y.append(jnp.concatenate([v[:per] for v in got], axis=0))
            dx.append(jnp.concatenate([v[per:] for v in got], axis=0))
        y, dx = (jnp.concatenate(v, axis=1).astype(BF16) for v in (y, dx))
        dxf = dx.astype(F32)
        inner = jnp.sum(dxf * a_ref[...], axis=1, keepdims=True)
        x = x_ref[...]
        combine = c_ref[...]
        dispatch = d_ref[...]
        d_combine = dot(y, g_ref[...], 1, 1)
        d_c = combine * (d_combine - jnp.sum(combine * d_combine, axis=0, keepdims=True))
        d_d = dispatch * (dot(dx, x, 1, 1) - inner)
        d_logit = (d_c + d_d).astype(BF16)
        d_route = dot(d_logit, x, 1, 0)
        l_ref[...] = d_logit
        y_ref[...] = y
        dx_ref[...] = dx
        for k in range(ns * ne):
            piece = d_route[:, k * cut : (k + 1) * cut]
            out[k] = jnp.concatenate([piece[: slots // 2], piece[slots // 2 :]], axis=1).astype(BF16)

    d_logit, y, dx, send = call(
        logit_kernel,
        [
            ((slots, length), BF16),
            ((slots, width), BF16),
            ((slots, width), BF16),
            ((ns * ne, slots // 2, 2 * cut), BF16),
        ],
        24,
        6 * slots * length * width,
        4 * length * width,
    )(rows_back, clip_rows, combine, dispatch, feats, cotangent)
    chunks = to_all(send)

    def token_products(combine, dispatch, d_logit, y, dx, route):
        left = jnp.concatenate([dispatch, d_logit.astype(F32)], axis=0).astype(BF16)
        right = jnp.concatenate([dx.astype(F32), route.astype(F32)], axis=0).astype(BF16)
        return (combine.astype(BF16), y), (left, right)

    mixed, d_feats, _ = outer(
        4, token_products, ((length, width),) * 2, combine, dispatch, d_logit, y, dx, router.T
    )

    def sum_kernel(in_ref, out_ref):
        full = jnp.sum(in_ref[...].astype(F32), axis=0)
        out_ref[...] = jnp.concatenate([full[:, :cut], full[:, cut:]], axis=0)

    (d_router,) = call(
        sum_kernel, [((slots, cut), F32)], 8, slots * width, slots * width * 4
    )(chunks)
    return mixed[None], d_feats[None], d_router.T, d_w_in[None], d_w_out[None]


def solution(mesh):
    in_specs = (
        P("exp", "seq", None),
        P(),
        P("exp", None, "seq"),
        P("exp", "seq", None),
        P("exp", "seq", None),
    )
    out_specs = (
        P("exp", "seq", None),
        P("exp", "seq", None),
        P(("seq", "exp"), None),
        P("exp", None, "seq"),
        P("exp", "seq", None),
    )
    body = functools.partial(shards, mesh.shape["seq"], mesh.shape["exp"])
    return jax.shard_map(body, mesh=mesh, in_specs=in_specs, out_specs=out_specs, check_vma=False)
```

```python
import functools
import math

import jax
import jax.numpy as jnp
from jax import lax
from jax.experimental import pallas as pl
from jax.experimental.pallas import tpu as pltpu
from jax.sharding import PartitionSpec as P

F32 = jnp.float32
BF16 = jnp.bfloat16
LANES = 128
FIRST_FLOPS = 1 << 40
PACK_MIB = 8
EXPERT_MIB = 24
PACK_FLOPS = 1 << 36
OUTER_FLOPS = 1 << 36
VMEM = pl.BlockSpec(memory_space=pltpu.VMEM)
HBM = pl.BlockSpec(memory_space=pltpu.HBM)


def dot(a, b, ca, cb):
    return lax.dot_general(a, b, (((ca,), (cb,)), ((), ())), preferred_element_type=F32)


def pieces(x):
    hi = x.astype(BF16)
    rest = x - hi.astype(F32)
    mid = rest.astype(BF16)
    return hi, mid, (rest - mid.astype(F32)).astype(BF16)


ERFC = (
    0.17087277, -0.82215223, 1.48851587, -1.13520398, 0.27886807,
    -0.18628806, 0.09678418, 0.37409196, 1.00002368, -1.26551223,
)


def gelu_parts(h):
    z = jnp.abs(h) * math.sqrt(0.5)
    t = 1.0 / (1.0 + 0.5 * z)
    poly = jnp.full_like(t, ERFC[0])
    for coefficient in ERFC[1:]:
        poly = poly * t + coefficient
    tail = 0.5 * t * jnp.exp(poly - z * z)
    cdf = jnp.where(h < 0, tail, 1.0 - tail)
    pdf = jnp.exp(-0.5 * h * h) * (1.0 / math.sqrt(2.0 * math.pi))
    return h * cdf, cdf + h * pdf


def call(body, out, vmem_mib, flops, nbytes, scratch=(), in_hbm=(), out_hbm=()):
    def run(*args):
        specs = [HBM if n in in_hbm else VMEM for n in range(len(args))]
        return pl.pallas_call(
            body,
            out_shape=tuple(jax.ShapeDtypeStruct(s, d) for s, d in out),
            in_specs=specs,
            out_specs=tuple(HBM if n in out_hbm else VMEM for n in range(len(out))),
            scratch_shapes=list(scratch),
            compiler_params=pltpu.CompilerParams(vmem_limit_bytes=int(vmem_mib * 2**20)),
            cost_estimate=pl.CostEstimate(flops=flops, bytes_accessed=nbytes, transcendentals=0),
        )(*args)

    return run


def shards(ns, ne, tokens, router, w_in, w_out, grad_out):
    feats, cotangent, w1, w2 = tokens[0], grad_out[0], w_in[0], w_out[0]
    length, width = feats.shape
    slots = router.shape[1]
    per = slots // ne
    hidden_part = w1.shape[1]
    half = width // 2
    wide = width + LANES
    cut = width // (ns * ne)

    def to_seq(x, k):
        return lax.ppermute(x, "seq", [(i, i ^ k) for i in range(ns)])

    def to_all(x):
        return lax.all_to_all(x, ("seq", "exp"), 0, 0, tiled=True)

    def pairs_of(a, b, n):
        at = slice(n * per, (n + 1) * per)
        return jnp.concatenate([a[at], b[at]], axis=0).astype(BF16)

    def stat_tile(*columns):
        lane = lax.broadcasted_iota(jnp.int32, (slots, LANES), 1)
        tile = jnp.zeros((slots, LANES), F32)
        for n, v in enumerate(columns):
            tile = jnp.where(lane == n, v.astype(F32), tile)
        return tile

    def first_kernel(out_ref):
        out_ref[...] = jnp.zeros((8, LANES), F32)

    (begun,) = call(first_kernel, [((8, LANES), F32)], 8, FIRST_FLOPS, 0)()

    def token_kernel(x_ref, r_ref, _, part_ref, combine_ref):
        x = x_ref[...]
        logits = dot(r_ref[...], x, 1, 1)
        top = jnp.max(logits, axis=1, keepdims=True)
        p = jnp.exp(logits - top)
        p_b = p.astype(BF16)
        total = jnp.sum(p, axis=1, keepdims=True)
        total_b = jnp.sum(p_b.astype(F32), axis=1, keepdims=True)
        e = jnp.exp(logits - jnp.max(logits, axis=0, keepdims=True))
        combine_ref[...] = (e / jnp.sum(e, axis=0, keepdims=True)).astype(BF16)
        part_ref[:, :width] = dot(p_b, x, 1, 0)
        part_ref[:, width:] = stat_tile(top, total, total_b)

    part, combine_b = call(
        token_kernel,
        [((slots, wide), F32), ((slots, length), BF16)],
        24,
        4 * slots * length * width,
        2 * length * width,
        in_hbm=(2,),
    )(feats, router.T, begun)

    def cotangent_kernel(p_ref, c_ref, g_ref, part_ref, keep_ref, half_ref):
        part_ref[:, :wide] = p_ref[...]
        b = dot(c_ref[...], g_ref[...], 1, 0)
        half_ref[0] = b[:, :half]
        half_ref[1] = b[:, half:]
        core = lax.rem(lax.axis_index("seq"), 2)
        part_ref[:, wide:] = half_ref[1 - core]
        keep_ref[...] = half_ref[core]

    part, keep = call(
        cotangent_kernel,
        [((slots, wide + half), F32), ((slots, half), F32)],
        24,
        2 * slots * length * width,
        2 * length * width,
        [pltpu.VMEM((2, slots, half), F32)],
    )(part, combine_b, cotangent)

    def merged(l_ref, r_ref):
        tops, totals, totals_b = (
            [r[:, width + n : width + n + 1] for r in (l_ref, r_ref)] for n in range(3)
        )
        top = jnp.maximum(*tops)
        scale = [jnp.exp(m - top) for m in tops]
        total, total_b = (scale[0] * v[0] + scale[1] * v[1] for v in (totals, totals_b))
        return scale[0] * l_ref[:, :width] + scale[1] * r_ref[:, :width], top, total, total_b

    def pack_kernel(l_ref, r_ref, keep_ref, part_ref, send_ref, half_ref):
        a, top, total, total_b = merged(l_ref, r_ref)
        part_ref[:, :width] = a
        part_ref[:, width:] = stat_tile(top, total, total_b)
        half_ref[0] = a[:, :half]
        half_ref[1] = a[:, half:]
        a = half_ref[lax.rem(lax.axis_index("seq"), 2)]
        b = keep_ref[...] + r_ref[:, wide:]
        rows = jnp.concatenate([a, b, stat_tile(*pieces(top), *pieces(total_b))], axis=1)
        for e in range(ne):
            chunk = rows[e * per : (e + 1) * per].astype(BF16)
            for s in range(ns):
                send_ref[s * ne + e] = chunk

    part, send = call(
        pack_kernel,
        [((slots, wide), F32), ((ns * ne, per, wide), BF16)],
        PACK_MIB,
        PACK_FLOPS,
        8 * slots * wide,
        [pltpu.VMEM((2, slots, half), F32)],
    )(part, to_seq(part, 1), keep)
    rows_in = to_all(send)

    def expert_kernel(*refs):
        w2_ref, in_ref, w1_ref, x_ref, dy_ref, act_ref, dh_ref, out_ref, keep_ref, *scratch = refs
        (half_ref,) = scratch
        tops, totals = [], []
        for s in range(0, ns, 2):
            tile = jnp.concatenate(
                [in_ref[s * ne + c, :, width:].astype(F32) for c in range(ne)], axis=0
            )
            tops.append(tile[:, 0:1] + tile[:, 1:2] + tile[:, 2:3])
            totals.append(tile[:, 3:4] + tile[:, 4:5] + tile[:, 5:6])
        top = functools.reduce(jnp.maximum, tops)
        scale = [jnp.exp(m - top) for m in tops]
        total = sum(w * v for w, v in zip(scale, totals))
        scale = [w / total for w in scale]
        xs, dys = [[], []], [[], []]
        for core in range(2):
            for c in range(ne):
                at = slice(c * per, (c + 1) * per)
                x, dy = 0.0, 0.0
                for w, s in zip(scale, range(core, ns, 2)):
                    x += w[at] * in_ref[s * ne + c, :, :half].astype(F32)
                    dy += in_ref[s * ne + c, :, half:width].astype(F32)
                xs[core].append(x)
                dys[core].append(dy)
        x, dy = (
            jnp.concatenate([jnp.concatenate(v, axis=0) for v in side], axis=1).astype(BF16)
            for side in (xs, dys)
        )
        x_ref[...] = x
        dy_ref[...] = dy
        w2v = w2_ref[...]
        d_act = dot(dy, w2v, 1, 1)
        act, slope = gelu_parts(dot(x, w1_ref[...], 1, 0))
        act = act.astype(BF16)
        act_ref[...] = act
        dh = (d_act * slope).astype(BF16)
        dh_ref[...] = dh
        y = dot(act, w2v, 1, 0)
        dx = dot(dh, w1_ref[...], 1, 1)
        for core in range(2):
            at = slice(core * half, (core + 1) * half)
            half_ref[core, :slots] = y[:, at]
            half_ref[core, slots:] = dx[:, at]
        core = lax.rem(lax.axis_index("seq"), 2)
        out_ref[...] = half_ref[1 - core]
        keep_ref[...] = half_ref[core]

    x_rows, dy_rows, act, dh, out, keep = call(
        expert_kernel,
        [((slots, width), BF16)] * 2
        + [((slots, hidden_part), BF16)] * 2
        + [((2 * slots, half), F32)] * 2,
        EXPERT_MIB,
        8 * slots * width * hidden_part,
        4 * width * hidden_part,
        [
            pltpu.VMEM((2, 2 * slots, half), F32),
        ],
    )(w2, rows_in, w1)

    def pack_back_kernel(l_ref, r_ref, send_hbm, near_ref, sems):
        full = l_ref[...] + r_ref[...]
        for c in range(ne):
            near_ref[c] = pairs_of(full[:slots], full[slots:], c)
        copies = [
            pltpu.make_async_copy(near_ref, send_hbm.at[pl.ds(s * ne, ne)], sems.at[s]) for s in range(ns)
        ]
        for copy in copies:
            copy.start()
        for copy in copies:
            copy.wait()

    (send,) = call(
        pack_back_kernel,
        [((ns * ne, 2 * per, half), BF16)],
        PACK_MIB,
        2 * slots * width,
        8 * slots * width,
        [pltpu.VMEM((ne, 2 * per, half), BF16), pltpu.SemaphoreType.DMA((ns,))],
        out_hbm=(0,),
    )(keep, to_seq(out, 1))
    rows_back = to_all(send)

    def outer(steps, build, shapes, *operands):
        def body(*refs):
            ins, outs, done_ref, near, sems = refs[:-6], refs[-6:-4], refs[-4], refs[-3:-1], refs[-1]
            pairs = build(*[r[...] for r in ins])
            copies = []
            for n in range(steps):
                for m, (left, right) in enumerate(pairs):
                    step = near[m].shape[0] // steps
                    at = slice(n * step, (n + 1) * step)
                    near[m][at] = dot(left[:, at], right, 0, 0).astype(BF16)
                    copy = pltpu.make_async_copy(near[m].at[at], outs[m].at[at], sems.at[2 * n + m])
                    copy.start()
                    copies.append(copy)
            done_ref[...] = jnp.zeros((8, LANES), F32)
            for copy in copies:
                copy.wait()

        return call(
            body,
            [(shape, BF16) for shape in shapes] + [((8, LANES), F32)],
            16,
            OUTER_FLOPS,
            sum(2 * m * n for m, n in shapes),
            [pltpu.VMEM(shape, BF16) for shape in shapes] + [pltpu.SemaphoreType.DMA((2 * steps,))],
            out_hbm=(0, 1),
        )(*operands)

    d_w_out, d_w_in, written = outer(
        5,
        lambda act, dy, x, dh: ((act, dy), (x, dh)),
        ((hidden_part, width), (width, hidden_part)),
        act,
        dy_rows,
        x_rows,
        dh,
    )

    def merge_kernel(l_ref, r_ref, out_ref):
        a, *stats = merged(l_ref, r_ref)
        out_ref[:, :width] = a
        out_ref[:, width:] = stat_tile(*stats)

    bits = (ns - 1).bit_length()
    for bit in range(1, bits - 1):
        (part,) = call(
            merge_kernel, [((slots, wide), F32)], 8, 4 * slots * width, 12 * slots * width
        )(part, to_seq(part, 1 << bit))

    def softmax_kernel(_, l_ref, r_ref, route_ref, x_ref, row_ref, combine_ref, dispatch_ref):
        a, top, total, total_b = merged(l_ref, r_ref)
        row_ref[...] = a / total_b
        logits = dot(route_ref[...], x_ref[...], 1, 1)
        e = jnp.exp(logits - jnp.max(logits, axis=0, keepdims=True))
        combine_ref[...] = e / jnp.sum(e, axis=0, keepdims=True)
        dispatch_ref[...] = jnp.exp(logits - top) / total

    clip_rows, combine, dispatch = call(
        softmax_kernel,
        [((slots, width), F32), ((slots, length), F32), ((slots, length), F32)],
        8,
        2 * slots * length * width,
        2 * length * width,
        in_hbm=(0,),
    )(written, part, to_seq(part, 1 << (bits - 1)), router.T, feats)

    def logit_kernel(in_ref, a_ref, c_ref, d_ref, x_ref, g_ref, l_ref, y_ref, dx_ref, out):
        y, dx = [], []
        for core in range(2):
            got = [sum(in_ref[s * ne + e].astype(F32) for s in range(core, ns, 2)) for e in range(ne)]
            y.append(jnp.concatenate([v[:per] for v in got], axis=0))
            dx.append(jnp.concatenate([v[per:] for v in got], axis=0))
        y, dx = (jnp.concatenate(v, axis=1).astype(BF16) for v in (y, dx))
        dxf = dx.astype(F32)
        inner = jnp.sum(dxf * a_ref[...], axis=1, keepdims=True)
        x = x_ref[...]
        combine = c_ref[...]
        dispatch = d_ref[...]
        d_combine = dot(y, g_ref[...], 1, 1)
        d_c = combine * (d_combine - jnp.sum(combine * d_combine, axis=0, keepdims=True))
        d_d = dispatch * (dot(dx, x, 1, 1) - inner)
        d_logit = (d_c + d_d).astype(BF16)
        d_route = dot(d_logit, x, 1, 0)
        l_ref[...] = d_logit
        y_ref[...] = y
        dx_ref[...] = dx
        for k in range(ns * ne):
            piece = d_route[:, k * cut : (k + 1) * cut]
            out[k] = jnp.concatenate([piece[: slots // 2], piece[slots // 2 :]], axis=1).astype(BF16)

    d_logit, y, dx, send = call(
        logit_kernel,
        [
            ((slots, length), BF16),
            ((slots, width), BF16),
            ((slots, width), BF16),
            ((ns * ne, slots // 2, 2 * cut), BF16),
        ],
        24,
        6 * slots * length * width,
        4 * length * width,
    )(rows_back, clip_rows, combine, dispatch, feats, cotangent)
    chunks = to_all(send)

    def token_products(combine, dispatch, d_logit, y, dx, route):
        left = jnp.concatenate([dispatch, d_logit.astype(F32)], axis=0).astype(BF16)
        right = jnp.concatenate([dx.astype(F32), route.astype(F32)], axis=0).astype(BF16)
        return (combine.astype(BF16), y), (left, right)

    mixed, d_feats, _ = outer(
        4, token_products, ((length, width),) * 2, combine, dispatch, d_logit, y, dx, router.T
    )

    def sum_kernel(in_ref, out_ref):
        full = jnp.sum(in_ref[...].astype(F32), axis=0)
        out_ref[...] = jnp.concatenate([full[:, :cut], full[:, cut:]], axis=0)

    (d_router,) = call(
        sum_kernel, [((slots, cut), F32)], 8, slots * width, slots * width * 4
    )(chunks)
    return mixed[None], d_feats[None], d_router.T, d_w_in[None], d_w_out[None]


def solution(mesh):
    in_specs = (
        P("exp", "seq", None),
        P(),
        P("exp", None, "seq"),
        P("exp", "seq", None),
        P("exp", "seq", None),
    )
    out_specs = (
        P("exp", "seq", None),
        P("exp", "seq", None),
        P(("seq", "exp"), None),
        P("exp", None, "seq"),
        P("exp", "seq", None),
    )
    body = functools.partial(shards, mesh.shape["seq"], mesh.shape["exp"])
    return jax.shard_map(body, mesh=mesh, in_specs=in_specs, out_specs=out_specs, check_vma=False)
```

```python
import functools
import math

import jax
import jax.numpy as jnp
from jax import lax
from jax.experimental import pallas as pl
from jax.experimental.pallas import tpu as pltpu
from jax.sharding import PartitionSpec as P

F32 = jnp.float32
BF16 = jnp.bfloat16
LANES = 128
FIRST_FLOPS = 1 << 40
PACK_MIB = 8
EXPERT_MIB = 24
PACK_FLOPS = 1 << 36
OUTER_FLOPS = 1 << 36
VMEM = pl.BlockSpec(memory_space=pltpu.VMEM)
HBM = pl.BlockSpec(memory_space=pltpu.HBM)


def dot(a, b, ca, cb):
    return lax.dot_general(a, b, (((ca,), (cb,)), ((), ())), preferred_element_type=F32)


def pieces(x):
    hi = x.astype(BF16)
    rest = x - hi.astype(F32)
    mid = rest.astype(BF16)
    return hi, mid, (rest - mid.astype(F32)).astype(BF16)


ERFC = (
    0.17087277, -0.82215223, 1.48851587, -1.13520398, 0.27886807,
    -0.18628806, 0.09678418, 0.37409196, 1.00002368, -1.26551223,
)


def gelu_parts(h):
    z = jnp.abs(h) * math.sqrt(0.5)
    t = 1.0 / (1.0 + 0.5 * z)
    poly = jnp.full_like(t, ERFC[0])
    for coefficient in ERFC[1:]:
        poly = poly * t + coefficient
    tail = 0.5 * t * jnp.exp(poly - z * z)
    cdf = jnp.where(h < 0, tail, 1.0 - tail)
    pdf = jnp.exp(-0.5 * h * h) * (1.0 / math.sqrt(2.0 * math.pi))
    return h * cdf, cdf + h * pdf


def call(body, out, vmem_mib, flops, nbytes, scratch=(), in_hbm=(), out_hbm=()):
    def run(*args):
        specs = [HBM if n in in_hbm else VMEM for n in range(len(args))]
        return pl.pallas_call(
            body,
            out_shape=tuple(jax.ShapeDtypeStruct(s, d) for s, d in out),
            in_specs=specs,
            out_specs=tuple(HBM if n in out_hbm else VMEM for n in range(len(out))),
            scratch_shapes=list(scratch),
            compiler_params=pltpu.CompilerParams(vmem_limit_bytes=int(vmem_mib * 2**20)),
            cost_estimate=pl.CostEstimate(flops=flops, bytes_accessed=nbytes, transcendentals=0),
        )(*args)

    return run


def shards(ns, ne, tokens, router, w_in, w_out, grad_out):
    feats, cotangent, w1, w2 = tokens[0], grad_out[0], w_in[0], w_out[0]
    length, width = feats.shape
    slots = router.shape[1]
    per = slots // ne
    hidden_part = w1.shape[1]
    half = width // 2
    wide = width + LANES
    cut = width // (ns * ne)

    def to_seq(x, k):
        return lax.ppermute(x, "seq", [(i, i ^ k) for i in range(ns)])

    def to_all(x):
        return lax.all_to_all(x, ("seq", "exp"), 0, 0, tiled=True)

    def stat_tile(*columns):
        lane = lax.broadcasted_iota(jnp.int32, (slots, LANES), 1)
        tile = jnp.zeros((slots, LANES), F32)
        for n, v in enumerate(columns):
            tile = jnp.where(lane == n, v.astype(F32), tile)
        return tile

    def first_kernel(out_ref):
        out_ref[...] = jnp.zeros((8, LANES), F32)

    (begun,) = call(first_kernel, [((8, LANES), F32)], 8, FIRST_FLOPS, 0)()

    def token_kernel(x_ref, r_ref, _, part_ref, combine_ref):
        x = x_ref[...]
        logits = dot(r_ref[...], x, 1, 1)
        top = jnp.max(logits, axis=1, keepdims=True)
        p = jnp.exp(logits - top)
        p_b = p.astype(BF16)
        total = jnp.sum(p, axis=1, keepdims=True)
        total_b = jnp.sum(p_b.astype(F32), axis=1, keepdims=True)
        e = jnp.exp(logits - jnp.max(logits, axis=0, keepdims=True))
        combine_ref[...] = (e / jnp.sum(e, axis=0, keepdims=True)).astype(BF16)
        part_ref[:, :width] = dot(p_b, x, 1, 0)
        part_ref[:, width:] = stat_tile(top, total, total_b)

    part, combine_b = call(
        token_kernel,
        [((slots, wide), F32), ((slots, length), BF16)],
        24,
        4 * slots * length * width,
        2 * length * width,
        in_hbm=(2,),
    )(feats, router.T, begun)

    def cotangent_kernel(p_ref, c_ref, g_ref, part_ref, keep_ref, half_ref):
        part_ref[:, :wide] = p_ref[...]
        b = dot(c_ref[...], g_ref[...], 1, 0)
        half_ref[0] = b[:, :half]
        half_ref[1] = b[:, half:]
        core = lax.rem(lax.axis_index("seq"), 2)
        part_ref[:, wide:] = half_ref[1 - core]
        keep_ref[...] = half_ref[core]

    part, keep = call(
        cotangent_kernel,
        [((slots, wide + half), F32), ((slots, half), F32)],
        24,
        2 * slots * length * width,
        2 * length * width,
        [pltpu.VMEM((2, slots, half), F32)],
    )(part, combine_b, cotangent)

    def merged(l_ref, r_ref):
        tops, totals, totals_b = (
            [r[:, width + n : width + n + 1] for r in (l_ref, r_ref)] for n in range(3)
        )
        top = jnp.maximum(*tops)
        scale = [jnp.exp(m - top) for m in tops]
        total, total_b = (scale[0] * v[0] + scale[1] * v[1] for v in (totals, totals_b))
        return scale[0] * l_ref[:, :width] + scale[1] * r_ref[:, :width], top, total, total_b

    def pack_kernel(l_ref, r_ref, keep_ref, part_ref, send_ref, half_ref):
        a, top, total, total_b = merged(l_ref, r_ref)
        part_ref[:, :width] = a
        part_ref[:, width:] = stat_tile(top, total, total_b)
        half_ref[0] = a[:, :half]
        half_ref[1] = a[:, half:]
        a = half_ref[lax.rem(lax.axis_index("seq"), 2)]
        b = keep_ref[...] + r_ref[:, wide:]
        rows = jnp.concatenate([a, b, stat_tile(*pieces(top), *pieces(total_b))], axis=1)
        for e in range(ne):
            chunk = rows[e * per : (e + 1) * per].astype(BF16)
            for s in range(ns):
                send_ref[s * ne + e] = chunk

    part, send = call(
        pack_kernel,
        [((slots, wide), F32), ((ns * ne, per, wide), BF16)],
        PACK_MIB,
        PACK_FLOPS,
        8 * slots * wide,
        [pltpu.VMEM((2, slots, half), F32)],
    )(part, to_seq(part, 1), keep)
    rows_in = to_all(send)

    def expert_kernel(*refs):
        w2_ref, in_ref, w1_ref, x_ref, dy_ref, act_ref, dh_ref, out_ref, keep_ref, *scratch = refs
        (half_ref,) = scratch
        tops, totals = [], []
        for s in range(0, ns, 2):
            tile = jnp.concatenate(
                [in_ref[s * ne + c, :, width:].astype(F32) for c in range(ne)], axis=0
            )
            tops.append(tile[:, 0:1] + tile[:, 1:2] + tile[:, 2:3])
            totals.append(tile[:, 3:4] + tile[:, 4:5] + tile[:, 5:6])
        top = functools.reduce(jnp.maximum, tops)
        scale = [jnp.exp(m - top) for m in tops]
        total = sum(w * v for w, v in zip(scale, totals))
        scale = [w / total for w in scale]
        xs, dys = [[], []], [[], []]
        for core in range(2):
            for c in range(ne):
                at = slice(c * per, (c + 1) * per)
                x, dy = 0.0, 0.0
                for w, s in zip(scale, range(core, ns, 2)):
                    x += w[at] * in_ref[s * ne + c, :, :half].astype(F32)
                    dy += in_ref[s * ne + c, :, half:width].astype(F32)
                xs[core].append(x)
                dys[core].append(dy)
        x, dy = (
            jnp.concatenate([jnp.concatenate(v, axis=0) for v in side], axis=1).astype(BF16)
            for side in (xs, dys)
        )
        x_ref[...] = x
        dy_ref[...] = dy
        w2v = w2_ref[...]
        d_act = dot(dy, w2v, 1, 1)
        act, slope = gelu_parts(dot(x, w1_ref[...], 1, 0))
        act = act.astype(BF16)
        act_ref[...] = act
        dh = (d_act * slope).astype(BF16)
        dh_ref[...] = dh
        y = dot(act, w2v, 1, 0)
        dx = dot(dh, w1_ref[...], 1, 1)
        for core in range(2):
            at = slice(core * half, (core + 1) * half)
            half_ref[core, :, :half] = y[:, at]
            half_ref[core, :, half:] = dx[:, at]
        core = lax.rem(lax.axis_index("seq"), 2)
        out_ref[...] = half_ref[1 - core]
        keep_ref[...] = half_ref[core]

    x_rows, dy_rows, act, dh, out, keep = call(
        expert_kernel,
        [((slots, width), BF16)] * 2
        + [((slots, hidden_part), BF16)] * 2
        + [((slots, width), F32)] * 2,
        EXPERT_MIB,
        8 * slots * width * hidden_part,
        4 * width * hidden_part,
        [
            pltpu.VMEM((2, slots, width), F32),
        ],
    )(w2, rows_in, w1)

    def pack_back_kernel(l_ref, r_ref, send_ref):
        full = l_ref[...] + r_ref[...]
        for c in range(ne):
            chunk = full[c * per : (c + 1) * per].astype(BF16)
            for s in range(ns):
                send_ref[s * ne + c] = chunk

    (send,) = call(
        pack_back_kernel,
        [((ns * ne, per, width), BF16)],
        PACK_MIB,
        2 * slots * width,
        8 * slots * width,
    )(keep, to_seq(out, 1))
    rows_back = to_all(send)

    def outer(steps, build, shapes, *operands):
        def body(*refs):
            ins, outs, done_ref, near, sems = refs[:-6], refs[-6:-4], refs[-4], refs[-3:-1], refs[-1]
            pairs = build(*[r[...] for r in ins])
            copies = []
            for n in range(steps):
                for m, (left, right) in enumerate(pairs):
                    step = near[m].shape[0] // steps
                    at = slice(n * step, (n + 1) * step)
                    near[m][at] = dot(left[:, at], right, 0, 0).astype(BF16)
                    copy = pltpu.make_async_copy(near[m].at[at], outs[m].at[at], sems.at[2 * n + m])
                    copy.start()
                    copies.append(copy)
            done_ref[...] = jnp.zeros((8, LANES), F32)
            for copy in copies:
                copy.wait()

        return call(
            body,
            [(shape, BF16) for shape in shapes] + [((8, LANES), F32)],
            16,
            OUTER_FLOPS,
            sum(2 * m * n for m, n in shapes),
            [pltpu.VMEM(shape, BF16) for shape in shapes] + [pltpu.SemaphoreType.DMA((2 * steps,))],
            out_hbm=(0, 1),
        )(*operands)

    d_w_out, d_w_in, written = outer(
        5,
        lambda act, dy, x, dh: ((act, dy), (x, dh)),
        ((hidden_part, width), (width, hidden_part)),
        act,
        dy_rows,
        x_rows,
        dh,
    )

    def merge_kernel(l_ref, r_ref, out_ref):
        a, *stats = merged(l_ref, r_ref)
        out_ref[:, :width] = a
        out_ref[:, width:] = stat_tile(*stats)

    bits = (ns - 1).bit_length()
    for bit in range(1, bits - 1):
        (part,) = call(
            merge_kernel, [((slots, wide), F32)], 8, 4 * slots * width, 12 * slots * width
        )(part, to_seq(part, 1 << bit))

    def softmax_kernel(_, l_ref, r_ref, route_ref, x_ref, row_ref, combine_ref, dispatch_ref):
        a, top, total, total_b = merged(l_ref, r_ref)
        row_ref[...] = a / total_b
        logits = dot(route_ref[...], x_ref[...], 1, 1)
        e = jnp.exp(logits - jnp.max(logits, axis=0, keepdims=True))
        combine_ref[...] = e / jnp.sum(e, axis=0, keepdims=True)
        dispatch_ref[...] = jnp.exp(logits - top) / total

    clip_rows, combine, dispatch = call(
        softmax_kernel,
        [((slots, width), F32), ((slots, length), F32), ((slots, length), F32)],
        8,
        2 * slots * length * width,
        2 * length * width,
        in_hbm=(0,),
    )(written, part, to_seq(part, 1 << (bits - 1)), router.T, feats)

    def logit_kernel(in_ref, a_ref, c_ref, d_ref, x_ref, g_ref, l_ref, y_ref, dx_ref, out):
        y, dx = [], []
        for core in range(2):
            got = [sum(in_ref[s * ne + e].astype(F32) for s in range(core, ns, 2)) for e in range(ne)]
            both = jnp.concatenate(got, axis=0)
            y.append(both[:, :half])
            dx.append(both[:, half:])
        y, dx = (jnp.concatenate(v, axis=1).astype(BF16) for v in (y, dx))
        dxf = dx.astype(F32)
        inner = jnp.sum(dxf * a_ref[...], axis=1, keepdims=True)
        x = x_ref[...]
        combine = c_ref[...]
        dispatch = d_ref[...]
        d_combine = dot(y, g_ref[...], 1, 1)
        d_c = combine * (d_combine - jnp.sum(combine * d_combine, axis=0, keepdims=True))
        d_d = dispatch * (dot(dx, x, 1, 1) - inner)
        d_logit = (d_c + d_d).astype(BF16)
        d_route = dot(d_logit, x, 1, 0)
        l_ref[...] = d_logit
        y_ref[...] = y
        dx_ref[...] = dx
        for k in range(ns * ne):
            piece = d_route[:, k * cut : (k + 1) * cut]
            out[k] = jnp.concatenate([piece[: slots // 2], piece[slots // 2 :]], axis=1).astype(BF16)

    d_logit, y, dx, send = call(
        logit_kernel,
        [
            ((slots, length), BF16),
            ((slots, width), BF16),
            ((slots, width), BF16),
            ((ns * ne, slots // 2, 2 * cut), BF16),
        ],
        24,
        6 * slots * length * width,
        4 * length * width,
    )(rows_back, clip_rows, combine, dispatch, feats, cotangent)
    chunks = to_all(send)

    def token_products(combine, dispatch, d_logit, y, dx, route):
        left = jnp.concatenate([dispatch, d_logit.astype(F32)], axis=0).astype(BF16)
        right = jnp.concatenate([dx.astype(F32), route.astype(F32)], axis=0).astype(BF16)
        return (combine.astype(BF16), y), (left, right)

    mixed, d_feats, _ = outer(
        4, token_products, ((length, width),) * 2, combine, dispatch, d_logit, y, dx, router.T
    )

    def sum_kernel(in_ref, out_ref):
        full = jnp.sum(in_ref[...].astype(F32), axis=0)
        out_ref[...] = jnp.concatenate([full[:, :cut], full[:, cut:]], axis=0)

    (d_router,) = call(
        sum_kernel, [((slots, cut), F32)], 8, slots * width, slots * width * 4
    )(chunks)
    return mixed[None], d_feats[None], d_router.T, d_w_in[None], d_w_out[None]


def solution(mesh):
    in_specs = (
        P("exp", "seq", None),
        P(),
        P("exp", None, "seq"),
        P("exp", "seq", None),
        P("exp", "seq", None),
    )
    out_specs = (
        P("exp", "seq", None),
        P("exp", "seq", None),
        P(("seq", "exp"), None),
        P("exp", None, "seq"),
        P("exp", "seq", None),
    )
    body = functools.partial(shards, mesh.shape["seq"], mesh.shape["exp"])
    return jax.shard_map(body, mesh=mesh, in_specs=in_specs, out_specs=out_specs, check_vma=False)
```

```python
import functools
import math

import jax
import jax.numpy as jnp
from jax import lax
from jax.experimental import pallas as pl
from jax.experimental.pallas import tpu as pltpu
from jax.sharding import PartitionSpec as P

F32 = jnp.float32
BF16 = jnp.bfloat16
LANES = 128
FIRST_FLOPS = 1 << 40
PACK_MIB = 8
EXPERT_MIB = 24
PACK_FLOPS = 1 << 36
OUTER_FLOPS = 1 << 36
VMEM = pl.BlockSpec(memory_space=pltpu.VMEM)
HBM = pl.BlockSpec(memory_space=pltpu.HBM)


def dot(a, b, ca, cb):
    return lax.dot_general(a, b, (((ca,), (cb,)), ((), ())), preferred_element_type=F32)


def pieces(x):
    hi = x.astype(BF16)
    rest = x - hi.astype(F32)
    mid = rest.astype(BF16)
    return hi, mid, (rest - mid.astype(F32)).astype(BF16)


ERFC = (
    0.17087277, -0.82215223, 1.48851587, -1.13520398, 0.27886807,
    -0.18628806, 0.09678418, 0.37409196, 1.00002368, -1.26551223,
)


def gelu_parts(h):
    z = jnp.abs(h) * math.sqrt(0.5)
    t = 1.0 / (1.0 + 0.5 * z)
    poly = jnp.full_like(t, ERFC[0])
    for coefficient in ERFC[1:]:
        poly = poly * t + coefficient
    tail = 0.5 * t * jnp.exp(poly - z * z)
    cdf = jnp.where(h < 0, tail, 1.0 - tail)
    pdf = jnp.exp(-0.5 * h * h) * (1.0 / math.sqrt(2.0 * math.pi))
    return h * cdf, cdf + h * pdf


def call(body, out, vmem_mib, flops, nbytes, scratch=(), in_hbm=(), out_hbm=()):
    def run(*args):
        specs = [HBM if n in in_hbm else VMEM for n in range(len(args))]
        return pl.pallas_call(
            body,
            out_shape=tuple(jax.ShapeDtypeStruct(s, d) for s, d in out),
            in_specs=specs,
            out_specs=tuple(HBM if n in out_hbm else VMEM for n in range(len(out))),
            scratch_shapes=list(scratch),
            compiler_params=pltpu.CompilerParams(vmem_limit_bytes=int(vmem_mib * 2**20)),
            cost_estimate=pl.CostEstimate(flops=flops, bytes_accessed=nbytes, transcendentals=0),
        )(*args)

    return run


def shards(ns, ne, tokens, router, w_in, w_out, grad_out):
    feats, cotangent, w1, w2 = tokens[0], grad_out[0], w_in[0], w_out[0]
    length, width = feats.shape
    slots = router.shape[1]
    per = slots // ne
    hidden_part = w1.shape[1]
    half = width // 2
    wide = width + LANES
    cut = width // (ns * ne)
    tile = pl.cdiv(2 * cut + 1, LANES) * LANES

    def to_seq(x, k):
        return lax.ppermute(x, "seq", [(i, i ^ k) for i in range(ns)])

    def to_all(x):
        return lax.all_to_all(x, ("seq", "exp"), 0, 0, tiled=True)

    def stat_tile(*columns):
        lane = lax.broadcasted_iota(jnp.int32, (slots, LANES), 1)
        tile = jnp.zeros((slots, LANES), F32)
        for n, v in enumerate(columns):
            tile = jnp.where(lane == n, v.astype(F32), tile)
        return tile

    def first_kernel(out_ref):
        out_ref[...] = jnp.zeros((8, LANES), F32)

    (begun,) = call(first_kernel, [((8, LANES), F32)], 8, FIRST_FLOPS, 0)()

    def token_kernel(x_ref, r_ref, _, part_ref, combine_ref):
        x = x_ref[...]
        logits = dot(r_ref[...], x, 1, 1)
        top = jnp.max(logits, axis=1, keepdims=True)
        p = jnp.exp(logits - top)
        p_b = p.astype(BF16)
        total = jnp.sum(p, axis=1, keepdims=True)
        total_b = jnp.sum(p_b.astype(F32), axis=1, keepdims=True)
        e = jnp.exp(logits - jnp.max(logits, axis=0, keepdims=True))
        combine_ref[...] = (e / jnp.sum(e, axis=0, keepdims=True)).astype(BF16)
        part_ref[:, :width] = dot(p_b, x, 1, 0)
        part_ref[:, width:] = stat_tile(top, total, total_b)

    part, combine_b = call(
        token_kernel,
        [((slots, wide), F32), ((slots, length), BF16)],
        24,
        4 * slots * length * width,
        2 * length * width,
        in_hbm=(2,),
    )(feats, router.T, begun)

    def cotangent_kernel(p_ref, c_ref, g_ref, part_ref, keep_ref, half_ref):
        part_ref[:, :wide] = p_ref[...]
        b = dot(c_ref[...], g_ref[...], 1, 0)
        half_ref[0] = b[:, :half]
        half_ref[1] = b[:, half:]
        core = lax.rem(lax.axis_index("seq"), 2)
        part_ref[:, wide:] = half_ref[1 - core]
        keep_ref[...] = half_ref[core]

    part, keep = call(
        cotangent_kernel,
        [((slots, wide + half), F32), ((slots, half), F32)],
        24,
        2 * slots * length * width,
        2 * length * width,
        [pltpu.VMEM((2, slots, half), F32)],
    )(part, combine_b, cotangent)

    def merged(l_ref, r_ref):
        tops, totals, totals_b = (
            [r[:, width + n : width + n + 1] for r in (l_ref, r_ref)] for n in range(3)
        )
        top = jnp.maximum(*tops)
        scale = [jnp.exp(m - top) for m in tops]
        total, total_b = (scale[0] * v[0] + scale[1] * v[1] for v in (totals, totals_b))
        return scale[0] * l_ref[:, :width] + scale[1] * r_ref[:, :width], top, total, total_b

    def pack_kernel(l_ref, r_ref, keep_ref, part_ref, send_ref, half_ref):
        a, top, total, total_b = merged(l_ref, r_ref)
        part_ref[:, :width] = a
        part_ref[:, width:] = stat_tile(top, total, total_b)
        half_ref[0] = a[:, :half]
        half_ref[1] = a[:, half:]
        a = half_ref[lax.rem(lax.axis_index("seq"), 2)]
        b = keep_ref[...] + r_ref[:, wide:]
        rows = jnp.concatenate([a, b, stat_tile(*pieces(top), *pieces(total_b))], axis=1)
        for e in range(ne):
            chunk = rows[e * per : (e + 1) * per].astype(BF16)
            for s in range(ns):
                send_ref[s * ne + e] = chunk

    part, send = call(
        pack_kernel,
        [((slots, wide), F32), ((ns * ne, per, wide), BF16)],
        PACK_MIB,
        PACK_FLOPS,
        8 * slots * wide,
        [pltpu.VMEM((2, slots, half), F32)],
    )(part, to_seq(part, 1), keep)
    rows_in = to_all(send)

    def expert_kernel(*refs):
        w2_ref, in_ref, w1_ref, x_ref, dy_ref, act_ref, dh_ref, out_ref, keep_ref, *scratch = refs
        (half_ref,) = scratch
        tops, totals = [], []
        for s in range(0, ns, 2):
            tile = jnp.concatenate(
                [in_ref[s * ne + c, :, width:].astype(F32) for c in range(ne)], axis=0
            )
            tops.append(tile[:, 0:1] + tile[:, 1:2] + tile[:, 2:3])
            totals.append(tile[:, 3:4] + tile[:, 4:5] + tile[:, 5:6])
        top = functools.reduce(jnp.maximum, tops)
        scale = [jnp.exp(m - top) for m in tops]
        total = sum(w * v for w, v in zip(scale, totals))
        scale = [w / total for w in scale]
        xs, dys = [[], []], [[], []]
        for core in range(2):
            for c in range(ne):
                at = slice(c * per, (c + 1) * per)
                x, dy = 0.0, 0.0
                for w, s in zip(scale, range(core, ns, 2)):
                    x += w[at] * in_ref[s * ne + c, :, :half].astype(F32)
                    dy += in_ref[s * ne + c, :, half:width].astype(F32)
                xs[core].append(x)
                dys[core].append(dy)
        x, dy = (
            jnp.concatenate([jnp.concatenate(v, axis=0) for v in side], axis=1).astype(BF16)
            for side in (xs, dys)
        )
        x_ref[...] = x
        dy_ref[...] = dy
        w2v = w2_ref[...]
        d_act = dot(dy, w2v, 1, 1)
        act, slope = gelu_parts(dot(x, w1_ref[...], 1, 0))
        act = act.astype(BF16)
        act_ref[...] = act
        dh = (d_act * slope).astype(BF16)
        dh_ref[...] = dh
        y = dot(act, w2v, 1, 0)
        dx = dot(dh, w1_ref[...], 1, 1)
        for core in range(2):
            at = slice(core * half, (core + 1) * half)
            half_ref[core, :, :half] = y[:, at]
            half_ref[core, :, half:] = dx[:, at]
        core = lax.rem(lax.axis_index("seq"), 2)
        out_ref[...] = half_ref[1 - core]
        keep_ref[...] = half_ref[core]

    x_rows, dy_rows, act, dh, out, keep = call(
        expert_kernel,
        [((slots, width), BF16)] * 2
        + [((slots, hidden_part), BF16)] * 2
        + [((slots, width), F32)] * 2,
        EXPERT_MIB,
        8 * slots * width * hidden_part,
        4 * width * hidden_part,
        [
            pltpu.VMEM((2, slots, width), F32),
        ],
    )(w2, rows_in, w1)

    def pack_back_kernel(l_ref, r_ref, send_ref):
        full = l_ref[...] + r_ref[...]
        for c in range(ne):
            chunk = full[c * per : (c + 1) * per].astype(BF16)
            for s in range(ns):
                send_ref[s * ne + c] = chunk

    (send,) = call(
        pack_back_kernel,
        [((ns * ne, per, width), BF16)],
        PACK_MIB,
        2 * slots * width,
        8 * slots * width,
    )(keep, to_seq(out, 1))
    rows_back = to_all(send)

    def outer(steps, build, shapes, *operands):
        def body(*refs):
            ins, outs, done_ref, near, sems = refs[:-6], refs[-6:-4], refs[-4], refs[-3:-1], refs[-1]
            pairs = build(*[r[...] for r in ins])
            copies = []
            for n in range(steps):
                for m, (left, right) in enumerate(pairs):
                    step = near[m].shape[0] // steps
                    at = slice(n * step, (n + 1) * step)
                    near[m][at] = dot(left[:, at], right, 0, 0).astype(BF16)
                    copy = pltpu.make_async_copy(near[m].at[at], outs[m].at[at], sems.at[2 * n + m])
                    copy.start()
                    copies.append(copy)
            done_ref[...] = jnp.zeros((8, LANES), F32)
            for copy in copies:
                copy.wait()

        return call(
            body,
            [(shape, BF16) for shape in shapes] + [((8, LANES), F32)],
            16,
            OUTER_FLOPS,
            sum(2 * m * n for m, n in shapes),
            [pltpu.VMEM(shape, BF16) for shape in shapes] + [pltpu.SemaphoreType.DMA((2 * steps,))],
            out_hbm=(0, 1),
        )(*operands)

    d_w_out, d_w_in, written = outer(
        5,
        lambda act, dy, x, dh: ((act, dy), (x, dh)),
        ((hidden_part, width), (width, hidden_part)),
        act,
        dy_rows,
        x_rows,
        dh,
    )

    def merge_kernel(l_ref, r_ref, out_ref):
        a, *stats = merged(l_ref, r_ref)
        out_ref[:, :width] = a
        out_ref[:, width:] = stat_tile(*stats)

    bits = (ns - 1).bit_length()
    for bit in range(1, bits - 1):
        (part,) = call(
            merge_kernel, [((slots, wide), F32)], 8, 4 * slots * width, 12 * slots * width
        )(part, to_seq(part, 1 << bit))

    def softmax_kernel(_, l_ref, r_ref, route_ref, x_ref, row_ref, combine_ref, dispatch_ref):
        a, top, total, total_b = merged(l_ref, r_ref)
        row_ref[...] = a / total_b
        logits = dot(route_ref[...], x_ref[...], 1, 1)
        e = jnp.exp(logits - jnp.max(logits, axis=0, keepdims=True))
        combine_ref[...] = e / jnp.sum(e, axis=0, keepdims=True)
        dispatch_ref[...] = jnp.exp(logits - top) / total

    clip_rows, combine, dispatch = call(
        softmax_kernel,
        [((slots, width), F32), ((slots, length), F32), ((slots, length), F32)],
        8,
        2 * slots * length * width,
        2 * length * width,
        in_hbm=(0,),
    )(written, part, to_seq(part, 1 << (bits - 1)), router.T, feats)

    def logit_kernel(in_ref, a_ref, c_ref, d_ref, x_ref, g_ref, l_ref, y_ref, dx_ref, out):
        y, dx = [], []
        for core in range(2):
            got = [sum(in_ref[s * ne + e].astype(F32) for s in range(core, ns, 2)) for e in range(ne)]
            both = jnp.concatenate(got, axis=0)
            y.append(both[:, :half])
            dx.append(both[:, half:])
        y, dx = (jnp.concatenate(v, axis=1).astype(BF16) for v in (y, dx))
        dxf = dx.astype(F32)
        inner = jnp.sum(dxf * a_ref[...], axis=1, keepdims=True)
        x = x_ref[...]
        combine = c_ref[...]
        dispatch = d_ref[...]
        d_combine = dot(y, g_ref[...], 1, 1)
        d_c = combine * (d_combine - jnp.sum(combine * d_combine, axis=0, keepdims=True))
        d_d = dispatch * (dot(dx, x, 1, 1) - inner)
        d_logit = (d_c + d_d).astype(BF16)
        d_route = dot(d_logit, x, 1, 0)
        l_ref[...] = d_logit
        y_ref[...] = y
        dx_ref[...] = dx
        fill = [jnp.zeros((slots // 2, tile - 2 * cut), F32)]
        for k in range(ns * ne):
            piece = d_route[:, k * cut : (k + 1) * cut]
            parts = [piece[: slots // 2], piece[slots // 2 :]] + fill
            out[k] = jnp.concatenate(parts, axis=1).astype(BF16)

    d_logit, y, dx, send = call(
        logit_kernel,
        [
            ((slots, length), BF16),
            ((slots, width), BF16),
            ((slots, width), BF16),
            ((ns * ne, slots // 2, tile), BF16),
        ],
        24,
        6 * slots * length * width,
        4 * length * width,
    )(rows_back, clip_rows, combine, dispatch, feats, cotangent)
    chunks = to_all(send)

    def token_products(combine, dispatch, d_logit, y, dx, route):
        left = jnp.concatenate([dispatch, d_logit.astype(F32)], axis=0).astype(BF16)
        right = jnp.concatenate([dx.astype(F32), route.astype(F32)], axis=0).astype(BF16)
        return (combine.astype(BF16), y), (left, right)

    mixed, d_feats, _ = outer(
        4, token_products, ((length, width),) * 2, combine, dispatch, d_logit, y, dx, router.T
    )

    def sum_kernel(in_ref, out_ref):
        full = jnp.sum(in_ref[...].astype(F32), axis=0)
        out_ref[...] = jnp.concatenate([full[:, :cut], full[:, cut : 2 * cut]], axis=0)

    (d_router,) = call(
        sum_kernel, [((slots, cut), F32)], 8, slots * width, slots * width * 4
    )(chunks)
    return mixed[None], d_feats[None], d_router.T, d_w_in[None], d_w_out[None]


def solution(mesh):
    in_specs = (
        P("exp", "seq", None),
        P(),
        P("exp", None, "seq"),
        P("exp", "seq", None),
        P("exp", "seq", None),
    )
    out_specs = (
        P("exp", "seq", None),
        P("exp", "seq", None),
        P(("seq", "exp"), None),
        P("exp", None, "seq"),
        P("exp", "seq", None),
    )
    body = functools.partial(shards, mesh.shape["seq"], mesh.shape["exp"])
    return jax.shard_map(body, mesh=mesh, in_specs=in_specs, out_specs=out_specs, check_vma=False)
```

```python
import functools
import math

import jax
import jax.numpy as jnp
from jax import lax
from jax.experimental import pallas as pl
from jax.experimental.pallas import tpu as pltpu
from jax.sharding import PartitionSpec as P

F32 = jnp.float32
BF16 = jnp.bfloat16
LANES = 128
FIRST_FLOPS = 1 << 40
PACK_MIB = 8
EXPERT_MIB = 24
PACK_FLOPS = 1 << 36
OUTER_FLOPS = 1 << 36
VMEM = pl.BlockSpec(memory_space=pltpu.VMEM)
HBM = pl.BlockSpec(memory_space=pltpu.HBM)


def dot(a, b, ca, cb):
    return lax.dot_general(a, b, (((ca,), (cb,)), ((), ())), preferred_element_type=F32)


def pieces(x):
    hi = x.astype(BF16)
    rest = x - hi.astype(F32)
    mid = rest.astype(BF16)
    return hi, mid, (rest - mid.astype(F32)).astype(BF16)


ERFC = (
    0.17087277, -0.82215223, 1.48851587, -1.13520398, 0.27886807,
    -0.18628806, 0.09678418, 0.37409196, 1.00002368, -1.26551223,
)


def gelu_parts(h):
    z = jnp.abs(h) * math.sqrt(0.5)
    t = 1.0 / (1.0 + 0.5 * z)
    poly = jnp.full_like(t, ERFC[0])
    for coefficient in ERFC[1:]:
        poly = poly * t + coefficient
    tail = 0.5 * t * jnp.exp(poly - z * z)
    cdf = jnp.where(h < 0, tail, 1.0 - tail)
    pdf = jnp.exp(-0.5 * h * h) * (1.0 / math.sqrt(2.0 * math.pi))
    return h * cdf, cdf + h * pdf


def call(body, out, vmem_mib, flops, nbytes, scratch=(), in_hbm=(), out_hbm=()):
    def run(*args):
        specs = [HBM if n in in_hbm else VMEM for n in range(len(args))]
        return pl.pallas_call(
            body,
            out_shape=tuple(jax.ShapeDtypeStruct(s, d) for s, d in out),
            in_specs=specs,
            out_specs=tuple(HBM if n in out_hbm else VMEM for n in range(len(out))),
            scratch_shapes=list(scratch),
            compiler_params=pltpu.CompilerParams(vmem_limit_bytes=int(vmem_mib * 2**20)),
            cost_estimate=pl.CostEstimate(flops=flops, bytes_accessed=nbytes, transcendentals=0),
        )(*args)

    return run


def shards(ns, ne, tokens, router, w_in, w_out, grad_out):
    feats, cotangent, w1, w2 = tokens[0], grad_out[0], w_in[0], w_out[0]
    length, width = feats.shape
    slots = router.shape[1]
    per = slots // ne
    hidden_part = w1.shape[1]
    half = width // 2
    wide = width + LANES
    cut = width // (ns * ne)

    def to_seq(x, k):
        return lax.ppermute(x, "seq", [(i, i ^ k) for i in range(ns)])

    def to_all(x):
        return lax.all_to_all(x, ("seq", "exp"), 0, 0, tiled=True)

    def stat_tile(*columns):
        lane = lax.broadcasted_iota(jnp.int32, (slots, LANES), 1)
        tile = jnp.zeros((slots, LANES), F32)
        for n, v in enumerate(columns):
            tile = jnp.where(lane == n, v.astype(F32), tile)
        return tile

    def first_kernel(out_ref):
        out_ref[...] = jnp.zeros((8, LANES), F32)

    (begun,) = call(first_kernel, [((8, LANES), F32)], 8, FIRST_FLOPS, 0)()

    def token_kernel(x_ref, r_ref, _, part_ref, combine_ref):
        x = x_ref[...]
        logits = dot(r_ref[...], x, 1, 1)
        top = jnp.max(logits, axis=1, keepdims=True)
        p = jnp.exp(logits - top)
        p_b = p.astype(BF16)
        part_ref[:, :width] = dot(p_b, x, 1, 0)
        total = jnp.sum(p, axis=1, keepdims=True)
        total_b = jnp.sum(p_b.astype(F32), axis=1, keepdims=True)
        e = jnp.exp(logits - jnp.max(logits, axis=0, keepdims=True))
        combine_ref[...] = (e / jnp.sum(e, axis=0, keepdims=True)).astype(BF16)
        part_ref[:, width:] = stat_tile(top, total, total_b)

    part, combine_b = call(
        token_kernel,
        [((slots, wide), F32), ((slots, length), BF16)],
        24,
        4 * slots * length * width,
        2 * length * width,
        in_hbm=(2,),
    )(feats, router.T, begun)

    def cotangent_kernel(p_ref, c_ref, g_ref, part_ref, keep_ref, half_ref):
        part_ref[:, :wide] = p_ref[...]
        b = dot(c_ref[...], g_ref[...], 1, 0)
        half_ref[0] = b[:, :half]
        half_ref[1] = b[:, half:]
        core = lax.rem(lax.axis_index("seq"), 2)
        part_ref[:, wide:] = half_ref[1 - core]
        keep_ref[...] = half_ref[core]

    part, keep = call(
        cotangent_kernel,
        [((slots, wide + half), F32), ((slots, half), F32)],
        24,
        2 * slots * length * width,
        2 * length * width,
        [pltpu.VMEM((2, slots, half), F32)],
    )(part, combine_b, cotangent)

    def merged(l_ref, r_ref):
        tops, totals, totals_b = (
            [r[:, width + n : width + n + 1] for r in (l_ref, r_ref)] for n in range(3)
        )
        top = jnp.maximum(*tops)
        scale = [jnp.exp(m - top) for m in tops]
        total, total_b = (scale[0] * v[0] + scale[1] * v[1] for v in (totals, totals_b))
        return scale[0] * l_ref[:, :width] + scale[1] * r_ref[:, :width], top, total, total_b

    def pack_kernel(l_ref, r_ref, keep_ref, part_ref, send_ref, half_ref):
        a, top, total, total_b = merged(l_ref, r_ref)
        part_ref[:, :width] = a
        part_ref[:, width:] = stat_tile(top, total, total_b)
        half_ref[0] = a[:, :half]
        half_ref[1] = a[:, half:]
        a = half_ref[lax.rem(lax.axis_index("seq"), 2)]
        b = keep_ref[...] + r_ref[:, wide:]
        rows = jnp.concatenate([a, b, stat_tile(*pieces(top), *pieces(total_b))], axis=1)
        for e in range(ne):
            chunk = rows[e * per : (e + 1) * per].astype(BF16)
            for s in range(ns):
                send_ref[s * ne + e] = chunk

    part, send = call(
        pack_kernel,
        [((slots, wide), F32), ((ns * ne, per, wide), BF16)],
        PACK_MIB,
        PACK_FLOPS,
        8 * slots * wide,
        [pltpu.VMEM((2, slots, half), F32)],
    )(part, to_seq(part, 1), keep)
    rows_in = to_all(send)

    def expert_kernel(*refs):
        w2_ref, in_ref, w1_ref, x_ref, dy_ref, act_ref, dh_ref, out_ref, keep_ref, *scratch = refs
        (half_ref,) = scratch
        dys = []
        for core in range(2):
            cut_rows = [
                sum(in_ref[s * ne + c, :, half:width].astype(F32) for s in range(core, ns, 2))
                for c in range(ne)
            ]
            dys.append(jnp.concatenate(cut_rows, axis=0))
        dy = jnp.concatenate(dys, axis=1).astype(BF16)
        w2v = w2_ref[...]
        d_act = dot(dy, w2v, 1, 1)
        tops, totals = [], []
        for s in range(0, ns, 2):
            tile = jnp.concatenate(
                [in_ref[s * ne + c, :, width:].astype(F32) for c in range(ne)], axis=0
            )
            tops.append(tile[:, 0:1] + tile[:, 1:2] + tile[:, 2:3])
            totals.append(tile[:, 3:4] + tile[:, 4:5] + tile[:, 5:6])
        top = functools.reduce(jnp.maximum, tops)
        scale = [jnp.exp(m - top) for m in tops]
        total = sum(w * v for w, v in zip(scale, totals))
        scale = [w / total for w in scale]
        xs = []
        for core in range(2):
            cut_rows = []
            for c in range(ne):
                at = slice(c * per, (c + 1) * per)
                cut_rows.append(
                    sum(
                        w[at] * in_ref[s * ne + c, :, :half].astype(F32)
                        for w, s in zip(scale, range(core, ns, 2))
                    )
                )
            xs.append(jnp.concatenate(cut_rows, axis=0))
        x = jnp.concatenate(xs, axis=1).astype(BF16)
        x_ref[...] = x
        dy_ref[...] = dy
        act, slope = gelu_parts(dot(x, w1_ref[...], 1, 0))
        act = act.astype(BF16)
        act_ref[...] = act
        dh = (d_act * slope).astype(BF16)
        dh_ref[...] = dh
        y = dot(act, w2v, 1, 0)
        dx = dot(dh, w1_ref[...], 1, 1)
        for core in range(2):
            at = slice(core * half, (core + 1) * half)
            half_ref[core, :, :half] = y[:, at]
            half_ref[core, :, half:] = dx[:, at]
        core = lax.rem(lax.axis_index("seq"), 2)
        out_ref[...] = half_ref[1 - core]
        keep_ref[...] = half_ref[core]

    x_rows, dy_rows, act, dh, out, keep = call(
        expert_kernel,
        [((slots, width), BF16)] * 2
        + [((slots, hidden_part), BF16)] * 2
        + [((slots, width), F32)] * 2,
        EXPERT_MIB,
        8 * slots * width * hidden_part,
        4 * width * hidden_part,
        [
            pltpu.VMEM((2, slots, width), F32),
        ],
    )(w2, rows_in, w1)

    def pack_back_kernel(l_ref, r_ref, send_ref):
        full = l_ref[...] + r_ref[...]
        for c in range(ne):
            chunk = full[c * per : (c + 1) * per].astype(BF16)
            for s in range(ns):
                send_ref[s * ne + c] = chunk

    (send,) = call(
        pack_back_kernel,
        [((ns * ne, per, width), BF16)],
        PACK_MIB,
        2 * slots * width,
        8 * slots * width,
    )(keep, to_seq(out, 1))
    rows_back = to_all(send)

    def outer(steps, build, shapes, *operands):
        def body(*refs):
            ins, outs, done_ref, near, sems = refs[:-6], refs[-6:-4], refs[-4], refs[-3:-1], refs[-1]
            pairs = build(*[r[...] for r in ins])
            copies = []
            for n in range(steps):
                for m, (left, right) in enumerate(pairs):
                    step = near[m].shape[0] // steps
                    at = slice(n * step, (n + 1) * step)
                    near[m][at] = dot(left[:, at], right, 0, 0).astype(BF16)
                    copy = pltpu.make_async_copy(near[m].at[at], outs[m].at[at], sems.at[2 * n + m])
                    copy.start()
                    copies.append(copy)
            done_ref[...] = jnp.zeros((8, LANES), F32)
            for copy in copies:
                copy.wait()

        return call(
            body,
            [(shape, BF16) for shape in shapes] + [((8, LANES), F32)],
            16,
            OUTER_FLOPS,
            sum(2 * m * n for m, n in shapes),
            [pltpu.VMEM(shape, BF16) for shape in shapes] + [pltpu.SemaphoreType.DMA((2 * steps,))],
            out_hbm=(0, 1),
        )(*operands)

    d_w_out, d_w_in, written = outer(
        5,
        lambda act, dy, x, dh: ((act, dy), (x, dh)),
        ((hidden_part, width), (width, hidden_part)),
        act,
        dy_rows,
        x_rows,
        dh,
    )

    def merge_kernel(l_ref, r_ref, out_ref):
        a, *stats = merged(l_ref, r_ref)
        out_ref[:, :width] = a
        out_ref[:, width:] = stat_tile(*stats)

    bits = (ns - 1).bit_length()
    for bit in range(1, bits - 1):
        (part,) = call(
            merge_kernel, [((slots, wide), F32)], 8, 4 * slots * width, 12 * slots * width
        )(part, to_seq(part, 1 << bit))

    def softmax_kernel(_, l_ref, r_ref, route_ref, x_ref, row_ref, combine_ref, dispatch_ref):
        a, top, total, total_b = merged(l_ref, r_ref)
        row_ref[...] = a / total_b
        logits = dot(route_ref[...], x_ref[...], 1, 1)
        e = jnp.exp(logits - jnp.max(logits, axis=0, keepdims=True))
        combine_ref[...] = e / jnp.sum(e, axis=0, keepdims=True)
        dispatch_ref[...] = jnp.exp(logits - top) / total

    clip_rows, combine, dispatch = call(
        softmax_kernel,
        [((slots, width), F32), ((slots, length), F32), ((slots, length), F32)],
        8,
        2 * slots * length * width,
        2 * length * width,
        in_hbm=(0,),
    )(written, part, to_seq(part, 1 << (bits - 1)), router.T, feats)

    def logit_kernel(in_ref, a_ref, c_ref, d_ref, x_ref, g_ref, l_ref, y_ref, dx_ref, out):
        def rows(at):
            sides = []
            for core in range(2):
                got = [
                    sum(in_ref[s * ne + e, :, at].astype(F32) for s in range(core, ns, 2))
                    for e in range(ne)
                ]
                sides.append(jnp.concatenate(got, axis=0))
            return jnp.concatenate(sides, axis=1).astype(BF16)

        y = rows(slice(0, half))
        d_combine = dot(y, g_ref[...], 1, 1)
        dx = rows(slice(half, width))
        x = x_ref[...]
        d_dispatch = dot(dx, x, 1, 1)
        dxf = dx.astype(F32)
        inner = jnp.sum(dxf * a_ref[...], axis=1, keepdims=True)
        combine = c_ref[...]
        dispatch = d_ref[...]
        d_c = combine * (d_combine - jnp.sum(combine * d_combine, axis=0, keepdims=True))
        d_d = dispatch * (d_dispatch - inner)
        d_logit = (d_c + d_d).astype(BF16)
        d_route = dot(d_logit, x, 1, 0)
        l_ref[...] = d_logit
        y_ref[...] = y
        dx_ref[...] = dx
        for k in range(ns * ne):
            piece = d_route[:, k * cut : (k + 1) * cut]
            out[k] = jnp.concatenate([piece[: slots // 2], piece[slots // 2 :]], axis=1).astype(BF16)

    d_logit, y, dx, send = call(
        logit_kernel,
        [
            ((slots, length), BF16),
            ((slots, width), BF16),
            ((slots, width), BF16),
            ((ns * ne, slots // 2, 2 * cut), BF16),
        ],
        24,
        6 * slots * length * width,
        4 * length * width,
    )(rows_back, clip_rows, combine, dispatch, feats, cotangent)
    chunks = to_all(send)

    def token_products(combine, dispatch, d_logit, y, dx, route):
        left = jnp.concatenate([dispatch, d_logit.astype(F32)], axis=0).astype(BF16)
        right = jnp.concatenate([dx.astype(F32), route.astype(F32)], axis=0).astype(BF16)
        return (combine.astype(BF16), y), (left, right)

    mixed, d_feats, _ = outer(
        4, token_products, ((length, width),) * 2, combine, dispatch, d_logit, y, dx, router.T
    )

    def sum_kernel(in_ref, out_ref):
        full = jnp.sum(in_ref[...].astype(F32), axis=0)
        out_ref[...] = jnp.concatenate([full[:, :cut], full[:, cut:]], axis=0)

    (d_router,) = call(
        sum_kernel, [((slots, cut), F32)], 8, slots * width, slots * width * 4
    )(chunks)
    return mixed[None], d_feats[None], d_router.T, d_w_in[None], d_w_out[None]


def solution(mesh):
    in_specs = (
        P("exp", "seq", None),
        P(),
        P("exp", None, "seq"),
        P("exp", "seq", None),
        P("exp", "seq", None),
    )
    out_specs = (
        P("exp", "seq", None),
        P("exp", "seq", None),
        P(("seq", "exp"), None),
        P("exp", None, "seq"),
        P("exp", "seq", None),
    )
    body = functools.partial(shards, mesh.shape["seq"], mesh.shape["exp"])
    return jax.shard_map(body, mesh=mesh, in_specs=in_specs, out_specs=out_specs, check_vma=False)
```

```python
import functools
import math

import jax
import jax.numpy as jnp
from jax import lax
from jax.experimental import pallas as pl
from jax.experimental.pallas import tpu as pltpu
from jax.sharding import PartitionSpec as P

F32 = jnp.float32
BF16 = jnp.bfloat16
LANES = 128
FIRST_FLOPS = 1 << 40
PACK_MIB = 8
EXPERT_MIB = 24
PACK_FLOPS = 1 << 36
OUTER_FLOPS = 1 << 36
VMEM = pl.BlockSpec(memory_space=pltpu.VMEM)
HBM = pl.BlockSpec(memory_space=pltpu.HBM)


def dot(a, b, ca, cb):
    return lax.dot_general(a, b, (((ca,), (cb,)), ((), ())), preferred_element_type=F32)


def pieces(x):
    hi = x.astype(BF16)
    rest = x - hi.astype(F32)
    mid = rest.astype(BF16)
    return hi, mid, (rest - mid.astype(F32)).astype(BF16)


ERFC = (
    0.17087277, -0.82215223, 1.48851587, -1.13520398, 0.27886807,
    -0.18628806, 0.09678418, 0.37409196, 1.00002368, -1.26551223,
)


def gelu_parts(h):
    z = jnp.abs(h) * math.sqrt(0.5)
    t = 1.0 / (1.0 + 0.5 * z)
    poly = jnp.full_like(t, ERFC[0])
    for coefficient in ERFC[1:]:
        poly = poly * t + coefficient
    tail = 0.5 * t * jnp.exp(poly - z * z)
    cdf = jnp.where(h < 0, tail, 1.0 - tail)
    pdf = jnp.exp(-0.5 * h * h) * (1.0 / math.sqrt(2.0 * math.pi))
    return h * cdf, cdf + h * pdf


def call(body, out, vmem_mib, flops, nbytes, scratch=(), in_hbm=(), out_hbm=()):
    def run(*args):
        specs = [HBM if n in in_hbm else VMEM for n in range(len(args))]
        return pl.pallas_call(
            body,
            out_shape=tuple(jax.ShapeDtypeStruct(s, d) for s, d in out),
            in_specs=specs,
            out_specs=tuple(HBM if n in out_hbm else VMEM for n in range(len(out))),
            scratch_shapes=list(scratch),
            compiler_params=pltpu.CompilerParams(vmem_limit_bytes=int(vmem_mib * 2**20)),
            cost_estimate=pl.CostEstimate(flops=flops, bytes_accessed=nbytes, transcendentals=0),
        )(*args)

    return run


def shards(ns, ne, tokens, router, w_in, w_out, grad_out):
    feats, cotangent, w1, w2 = tokens[0], grad_out[0], w_in[0], w_out[0]
    length, width = feats.shape
    slots = router.shape[1]
    per = slots // ne
    hidden_part = w1.shape[1]
    half = width // 2
    wide = width + LANES
    cut = width // (ns * ne)

    def to_seq(x, k):
        return lax.ppermute(x, "seq", [(i, i ^ k) for i in range(ns)])

    def to_all(x):
        return lax.all_to_all(x, ("seq", "exp"), 0, 0, tiled=True)

    def stat_tile(*columns):
        lane = lax.broadcasted_iota(jnp.int32, (slots, LANES), 1)
        tile = jnp.zeros((slots, LANES), F32)
        for n, v in enumerate(columns):
            tile = jnp.where(lane == n, v.astype(F32), tile)
        return tile

    def first_kernel(out_ref):
        out_ref[...] = jnp.zeros((8, LANES), F32)

    (begun,) = call(first_kernel, [((8, LANES), F32)], 8, FIRST_FLOPS, 0)()

    def token_kernel(x_ref, r_ref, _, part_ref, combine_ref):
        x = x_ref[...]
        logits = dot(r_ref[...], x, 1, 1)
        top = jnp.max(logits, axis=1, keepdims=True)
        p = jnp.exp(logits - top)
        p_b = p.astype(BF16)
        total = jnp.sum(p, axis=1, keepdims=True)
        total_b = jnp.sum(p_b.astype(F32), axis=1, keepdims=True)
        e = jnp.exp(logits - jnp.max(logits, axis=0, keepdims=True))
        combine_ref[...] = (e / jnp.sum(e, axis=0, keepdims=True)).astype(BF16)
        part_ref[:, :width] = dot(p_b, x, 1, 0)
        part_ref[:, width:] = stat_tile(top, total, total_b)

    part, combine_b = call(
        token_kernel,
        [((slots, wide), F32), ((slots, length), BF16)],
        24,
        4 * slots * length * width,
        2 * length * width,
        in_hbm=(2,),
    )(feats, router.T, begun)

    def cotangent_kernel(c_ref, g_ref, out_ref, keep_ref, half_ref):
        b = dot(c_ref[...], g_ref[...], 1, 0)
        half_ref[0] = b[:, :half]
        half_ref[1] = b[:, half:]
        core = lax.rem(lax.axis_index("seq"), 2)
        out_ref[...] = half_ref[1 - core]
        keep_ref[...] = half_ref[core]

    out, keep = call(
        cotangent_kernel,
        [((slots, half), F32)] * 2,
        24,
        2 * slots * length * width,
        2 * length * width,
        [pltpu.VMEM((2, slots, half), F32)],
    )(combine_b, cotangent)

    def merged(l_ref, r_ref):
        tops, totals, totals_b = (
            [r[:, width + n : width + n + 1] for r in (l_ref, r_ref)] for n in range(3)
        )
        top = jnp.maximum(*tops)
        scale = [jnp.exp(m - top) for m in tops]
        total, total_b = (scale[0] * v[0] + scale[1] * v[1] for v in (totals, totals_b))
        return scale[0] * l_ref[:, :width] + scale[1] * r_ref[:, :width], top, total, total_b

    def pack_kernel(l_ref, r_ref, keep_ref, their_ref, part_ref, send_ref, half_ref):
        a, top, total, total_b = merged(l_ref, r_ref)
        part_ref[:, :width] = a
        part_ref[:, width:] = stat_tile(top, total, total_b)
        half_ref[0] = a[:, :half]
        half_ref[1] = a[:, half:]
        a = half_ref[lax.rem(lax.axis_index("seq"), 2)]
        b = keep_ref[...] + their_ref[...]
        rows = jnp.concatenate([a, b, stat_tile(*pieces(top), *pieces(total_b))], axis=1)
        for e in range(ne):
            chunk = rows[e * per : (e + 1) * per].astype(BF16)
            for s in range(ns):
                send_ref[s * ne + e] = chunk

    part, send = call(
        pack_kernel,
        [((slots, wide), F32), ((ns * ne, per, wide), BF16)],
        PACK_MIB,
        PACK_FLOPS,
        8 * slots * wide,
        [pltpu.VMEM((2, slots, half), F32)],
    )(part, to_seq(part, 1), keep, to_seq(out, 1))
    rows_in = to_all(send)

    def expert_kernel(*refs):
        w2_ref, in_ref, w1_ref, x_ref, dy_ref, act_ref, dh_ref, out_ref, keep_ref, *scratch = refs
        (half_ref,) = scratch
        tops, totals = [], []
        for s in range(0, ns, 2):
            tile = jnp.concatenate(
                [in_ref[s * ne + c, :, width:].astype(F32) for c in range(ne)], axis=0
            )
            tops.append(tile[:, 0:1] + tile[:, 1:2] + tile[:, 2:3])
            totals.append(tile[:, 3:4] + tile[:, 4:5] + tile[:, 5:6])
        top = functools.reduce(jnp.maximum, tops)
        scale = [jnp.exp(m - top) for m in tops]
        total = sum(w * v for w, v in zip(scale, totals))
        scale = [w / total for w in scale]
        xs, dys = [[], []], [[], []]
        for core in range(2):
            for c in range(ne):
                at = slice(c * per, (c + 1) * per)
                x, dy = 0.0, 0.0
                for w, s in zip(scale, range(core, ns, 2)):
                    x += w[at] * in_ref[s * ne + c, :, :half].astype(F32)
                    dy += in_ref[s * ne + c, :, half:width].astype(F32)
                xs[core].append(x)
                dys[core].append(dy)
        x, dy = (
            jnp.concatenate([jnp.concatenate(v, axis=0) for v in side], axis=1).astype(BF16)
            for side in (xs, dys)
        )
        x_ref[...] = x
        dy_ref[...] = dy
        w2v = w2_ref[...]
        d_act = dot(dy, w2v, 1, 1)
        act, slope = gelu_parts(dot(x, w1_ref[...], 1, 0))
        act = act.astype(BF16)
        act_ref[...] = act
        dh = (d_act * slope).astype(BF16)
        dh_ref[...] = dh
        y = dot(act, w2v, 1, 0)
        dx = dot(dh, w1_ref[...], 1, 1)
        for core in range(2):
            at = slice(core * half, (core + 1) * half)
            half_ref[core, :, :half] = y[:, at]
            half_ref[core, :, half:] = dx[:, at]
        core = lax.rem(lax.axis_index("seq"), 2)
        out_ref[...] = half_ref[1 - core]
        keep_ref[...] = half_ref[core]

    x_rows, dy_rows, act, dh, out, keep = call(
        expert_kernel,
        [((slots, width), BF16)] * 2
        + [((slots, hidden_part), BF16)] * 2
        + [((slots, width), F32)] * 2,
        EXPERT_MIB,
        8 * slots * width * hidden_part,
        4 * width * hidden_part,
        [
            pltpu.VMEM((2, slots, width), F32),
        ],
    )(w2, rows_in, w1)

    def pack_back_kernel(l_ref, r_ref, send_ref):
        full = l_ref[...] + r_ref[...]
        for c in range(ne):
            chunk = full[c * per : (c + 1) * per].astype(BF16)
            for s in range(ns):
                send_ref[s * ne + c] = chunk

    (send,) = call(
        pack_back_kernel,
        [((ns * ne, per, width), BF16)],
        PACK_MIB,
        2 * slots * width,
        8 * slots * width,
    )(keep, to_seq(out, 1))
    rows_back = to_all(send)

    def outer(steps, build, shapes, *operands):
        def body(*refs):
            ins, outs, done_ref, near, sems = refs[:-6], refs[-6:-4], refs[-4], refs[-3:-1], refs[-1]
            pairs = build(*[r[...] for r in ins])
            copies = []
            for n in range(steps):
                for m, (left, right) in enumerate(pairs):
                    step = near[m].shape[0] // steps
                    at = slice(n * step, (n + 1) * step)
                    near[m][at] = dot(left[:, at], right, 0, 0).astype(BF16)
                    copy = pltpu.make_async_copy(near[m].at[at], outs[m].at[at], sems.at[2 * n + m])
                    copy.start()
                    copies.append(copy)
            done_ref[...] = jnp.zeros((8, LANES), F32)
            for copy in copies:
                copy.wait()

        return call(
            body,
            [(shape, BF16) for shape in shapes] + [((8, LANES), F32)],
            16,
            OUTER_FLOPS,
            sum(2 * m * n for m, n in shapes),
            [pltpu.VMEM(shape, BF16) for shape in shapes] + [pltpu.SemaphoreType.DMA((2 * steps,))],
            out_hbm=(0, 1),
        )(*operands)

    d_w_out, d_w_in, written = outer(
        5,
        lambda act, dy, x, dh: ((act, dy), (x, dh)),
        ((hidden_part, width), (width, hidden_part)),
        act,
        dy_rows,
        x_rows,
        dh,
    )

    def merge_kernel(l_ref, r_ref, out_ref):
        a, *stats = merged(l_ref, r_ref)
        out_ref[:, :width] = a
        out_ref[:, width:] = stat_tile(*stats)

    bits = (ns - 1).bit_length()
    for bit in range(1, bits - 1):
        (part,) = call(
            merge_kernel, [((slots, wide), F32)], 8, 4 * slots * width, 12 * slots * width
        )(part, to_seq(part, 1 << bit))

    def softmax_kernel(_, l_ref, r_ref, route_ref, x_ref, row_ref, combine_ref, dispatch_ref):
        a, top, total, total_b = merged(l_ref, r_ref)
        row_ref[...] = a / total_b
        logits = dot(route_ref[...], x_ref[...], 1, 1)
        e = jnp.exp(logits - jnp.max(logits, axis=0, keepdims=True))
        combine_ref[...] = e / jnp.sum(e, axis=0, keepdims=True)
        dispatch_ref[...] = jnp.exp(logits - top) / total

    clip_rows, combine, dispatch = call(
        softmax_kernel,
        [((slots, width), F32), ((slots, length), F32), ((slots, length), F32)],
        8,
        2 * slots * length * width,
        2 * length * width,
        in_hbm=(0,),
    )(written, part, to_seq(part, 1 << (bits - 1)), router.T, feats)

    def logit_kernel(in_ref, a_ref, c_ref, d_ref, x_ref, g_ref, l_ref, y_ref, dx_ref, out):
        y, dx = [], []
        for core in range(2):
            got = [sum(in_ref[s * ne + e].astype(F32) for s in range(core, ns, 2)) for e in range(ne)]
            both = jnp.concatenate(got, axis=0)
            y.append(both[:, :half])
            dx.append(both[:, half:])
        y, dx = (jnp.concatenate(v, axis=1).astype(BF16) for v in (y, dx))
        dxf = dx.astype(F32)
        inner = jnp.sum(dxf * a_ref[...], axis=1, keepdims=True)
        x = x_ref[...]
        combine = c_ref[...]
        dispatch = d_ref[...]
        d_combine = dot(y, g_ref[...], 1, 1)
        d_c = combine * (d_combine - jnp.sum(combine * d_combine, axis=0, keepdims=True))
        d_d = dispatch * (dot(dx, x, 1, 1) - inner)
        d_logit = (d_c + d_d).astype(BF16)
        d_route = dot(d_logit, x, 1, 0)
        l_ref[...] = d_logit
        y_ref[...] = y
        dx_ref[...] = dx
        for k in range(ns * ne):
            piece = d_route[:, k * cut : (k + 1) * cut]
            out[k] = jnp.concatenate([piece[: slots // 2], piece[slots // 2 :]], axis=1).astype(BF16)

    d_logit, y, dx, send = call(
        logit_kernel,
        [
            ((slots, length), BF16),
            ((slots, width), BF16),
            ((slots, width), BF16),
            ((ns * ne, slots // 2, 2 * cut), BF16),
        ],
        24,
        6 * slots * length * width,
        4 * length * width,
    )(rows_back, clip_rows, combine, dispatch, feats, cotangent)
    chunks = to_all(send)

    def token_products(combine, dispatch, d_logit, y, dx, route):
        left = jnp.concatenate([dispatch, d_logit.astype(F32)], axis=0).astype(BF16)
        right = jnp.concatenate([dx.astype(F32), route.astype(F32)], axis=0).astype(BF16)
        return (combine.astype(BF16), y), (left, right)

    mixed, d_feats, _ = outer(
        4, token_products, ((length, width),) * 2, combine, dispatch, d_logit, y, dx, router.T
    )

    def sum_kernel(in_ref, out_ref):
        full = jnp.sum(in_ref[...].astype(F32), axis=0)
        out_ref[...] = jnp.concatenate([full[:, :cut], full[:, cut:]], axis=0)

    (d_router,) = call(
        sum_kernel, [((slots, cut), F32)], 8, slots * width, slots * width * 4
    )(chunks)
    return mixed[None], d_feats[None], d_router.T, d_w_in[None], d_w_out[None]


def solution(mesh):
    in_specs = (
        P("exp", "seq", None),
        P(),
        P("exp", None, "seq"),
        P("exp", "seq", None),
        P("exp", "seq", None),
    )
    out_specs = (
        P("exp", "seq", None),
        P("exp", "seq", None),
        P(("seq", "exp"), None),
        P("exp", None, "seq"),
        P("exp", "seq", None),
    )
    body = functools.partial(shards, mesh.shape["seq"], mesh.shape["exp"])
    return jax.shard_map(body, mesh=mesh, in_specs=in_specs, out_specs=out_specs, check_vma=False)
```

```python
import functools
import math

import jax
import jax.numpy as jnp
from jax import lax
from jax.experimental import pallas as pl
from jax.experimental.pallas import tpu as pltpu
from jax.sharding import PartitionSpec as P

F32 = jnp.float32
BF16 = jnp.bfloat16
LANES = 128
FIRST_FLOPS = 1 << 40
PACK_MIB = 8
EXPERT_MIB = 24
PACK_FLOPS = 1 << 36
OUTER_FLOPS = 1 << 36
VMEM = pl.BlockSpec(memory_space=pltpu.VMEM)
HBM = pl.BlockSpec(memory_space=pltpu.HBM)


def dot(a, b, ca, cb):
    return lax.dot_general(a, b, (((ca,), (cb,)), ((), ())), preferred_element_type=F32)


def pieces(x):
    hi = x.astype(BF16)
    rest = x - hi.astype(F32)
    mid = rest.astype(BF16)
    return hi, mid, (rest - mid.astype(F32)).astype(BF16)


ERFC = (
    0.17087277, -0.82215223, 1.48851587, -1.13520398, 0.27886807,
    -0.18628806, 0.09678418, 0.37409196, 1.00002368, -1.26551223,
)


def gelu_parts(h):
    z = jnp.abs(h) * math.sqrt(0.5)
    t = 1.0 / (1.0 + 0.5 * z)
    poly = jnp.full_like(t, ERFC[0])
    for coefficient in ERFC[1:]:
        poly = poly * t + coefficient
    tail = 0.5 * t * jnp.exp(poly - z * z)
    cdf = jnp.where(h < 0, tail, 1.0 - tail)
    pdf = jnp.exp(-0.5 * h * h) * (1.0 / math.sqrt(2.0 * math.pi))
    return h * cdf, cdf + h * pdf


def call(body, out, vmem_mib, flops, nbytes, scratch=(), in_hbm=(), out_hbm=()):
    def run(*args):
        specs = [HBM if n in in_hbm else VMEM for n in range(len(args))]
        return pl.pallas_call(
            body,
            out_shape=tuple(jax.ShapeDtypeStruct(s, d) for s, d in out),
            in_specs=specs,
            out_specs=tuple(HBM if n in out_hbm else VMEM for n in range(len(out))),
            scratch_shapes=list(scratch),
            compiler_params=pltpu.CompilerParams(vmem_limit_bytes=int(vmem_mib * 2**20)),
            cost_estimate=pl.CostEstimate(flops=flops, bytes_accessed=nbytes, transcendentals=0),
        )(*args)

    return run


def shards(ns, ne, tokens, router, w_in, w_out, grad_out):
    feats, cotangent, w1, w2 = tokens[0], grad_out[0], w_in[0], w_out[0]
    length, width = feats.shape
    slots = router.shape[1]
    per = slots // ne
    hidden_part = w1.shape[1]
    half = width // 2
    wide = width + LANES
    cut = width // (ns * ne)

    def to_seq(x, k):
        return lax.ppermute(x, "seq", [(i, i ^ k) for i in range(ns)])

    def to_all(x):
        return lax.all_to_all(x, ("seq", "exp"), 0, 0, tiled=True)

    def stat_tile(*columns):
        lane = lax.broadcasted_iota(jnp.int32, (slots, LANES), 1)
        tile = jnp.zeros((slots, LANES), F32)
        for n, v in enumerate(columns):
            tile = jnp.where(lane == n, v.astype(F32), tile)
        return tile

    def first_kernel(out_ref):
        out_ref[...] = jnp.zeros((8, LANES), F32)

    (begun,) = call(first_kernel, [((8, LANES), F32)], 8, FIRST_FLOPS, 0)()

    def token_kernel(x_ref, r_ref, _, part_ref, combine_ref):
        x = x_ref[...]
        logits = dot(r_ref[...], x, 1, 1)
        top = jnp.max(logits, axis=1, keepdims=True)
        p = jnp.exp(logits - top)
        p_b = p.astype(BF16)
        total = jnp.sum(p, axis=1, keepdims=True)
        total_b = jnp.sum(p_b.astype(F32), axis=1, keepdims=True)
        e = jnp.exp(logits - jnp.max(logits, axis=0, keepdims=True))
        combine_ref[...] = (e / jnp.sum(e, axis=0, keepdims=True)).astype(BF16)
        part_ref[:, :width] = dot(p_b, x, 1, 0)
        part_ref[:, width:] = stat_tile(top, total, total_b)

    part, combine_b = call(
        token_kernel,
        [((slots, wide), F32), ((slots, length), BF16)],
        24,
        4 * slots * length * width,
        2 * length * width,
        in_hbm=(2,),
    )(feats, router.T, begun)

    def cotangent_kernel(p_ref, c_ref, g_ref, part_ref, keep_ref, half_ref):
        part_ref[:, :wide] = p_ref[...]
        b = dot(c_ref[...], g_ref[...], 1, 0)
        half_ref[0] = b[:, :half]
        half_ref[1] = b[:, half:]
        core = lax.rem(lax.axis_index("seq"), 2)
        part_ref[:, wide:] = half_ref[1 - core]
        keep_ref[...] = half_ref[core]

    part, keep = call(
        cotangent_kernel,
        [((slots, wide + half), F32), ((slots, half), F32)],
        24,
        2 * slots * length * width,
        2 * length * width,
        [pltpu.VMEM((2, slots, half), F32)],
    )(part, combine_b, cotangent)

    def merged(l_ref, r_ref):
        tops, totals, totals_b = (
            [r[:, width + n : width + n + 1] for r in (l_ref, r_ref)] for n in range(3)
        )
        top = jnp.maximum(*tops)
        scale = [jnp.exp(m - top) for m in tops]
        total, total_b = (scale[0] * v[0] + scale[1] * v[1] for v in (totals, totals_b))
        return scale[0] * l_ref[:, :width] + scale[1] * r_ref[:, :width], top, total, total_b

    def pack_kernel(l_ref, r_ref, keep_ref, part_ref, send_ref, half_ref):
        a, top, total, total_b = merged(l_ref, r_ref)
        part_ref[:, :width] = a
        part_ref[:, width:] = stat_tile(top, total, total_b)
        half_ref[0] = a[:, :half]
        half_ref[1] = a[:, half:]
        a = half_ref[lax.rem(lax.axis_index("seq"), 2)]
        b = keep_ref[...] + r_ref[:, wide:]
        rows = jnp.concatenate([a, b, stat_tile(*pieces(top), *pieces(total_b))], axis=1)
        for e in range(ne):
            chunk = rows[e * per : (e + 1) * per].astype(BF16)
            for s in range(ns):
                send_ref[s * ne + e] = chunk

    part, send = call(
        pack_kernel,
        [((slots, wide), F32), ((ns * ne, per, wide), BF16)],
        PACK_MIB,
        PACK_FLOPS,
        8 * slots * wide,
        [pltpu.VMEM((2, slots, half), F32)],
    )(part, to_seq(part, 1), keep)
    rows_in = to_all(send)

    def expert_kernel(*refs):
        w2_ref, in_ref, w1_ref, x_ref, dy_ref, act_ref, dh_ref, out_ref, keep_ref, *scratch = refs
        (half_ref,) = scratch
        tops, totals = [], []
        for s in range(0, ns, 2):
            tile = jnp.concatenate(
                [in_ref[s * ne + c, :, width:].astype(F32) for c in range(ne)], axis=0
            )
            tops.append(tile[:, 0:1] + tile[:, 1:2] + tile[:, 2:3])
            totals.append(tile[:, 3:4] + tile[:, 4:5] + tile[:, 5:6])
        top = functools.reduce(jnp.maximum, tops)
        scale = [jnp.exp(m - top) for m in tops]
        total = sum(w * v for w, v in zip(scale, totals))
        scale = [w / total for w in scale]
        xs, dys = [[], []], [[], []]
        for core in range(2):
            for c in range(ne):
                at = slice(c * per, (c + 1) * per)
                x, dy = 0.0, 0.0
                for w, s in zip(scale, range(core, ns, 2)):
                    x += w[at] * in_ref[s * ne + c, :, :half].astype(F32)
                    dy += in_ref[s * ne + c, :, half:width].astype(F32)
                xs[core].append(x)
                dys[core].append(dy)
        x, dy = (
            jnp.concatenate([jnp.concatenate(v, axis=0) for v in side], axis=1).astype(BF16)
            for side in (xs, dys)
        )
        x_ref[...] = x
        dy_ref[...] = dy
        w2v = w2_ref[...]
        d_act = dot(dy, w2v, 1, 1)
        act, slope = gelu_parts(dot(x, w1_ref[...], 1, 0))
        act = act.astype(BF16)
        act_ref[...] = act
        dh = (d_act * slope).astype(BF16)
        dh_ref[...] = dh
        y = dot(act, w2v, 1, 0)
        dx = dot(dh, w1_ref[...], 1, 1)
        for core in range(2):
            at = slice(core * half, (core + 1) * half)
            half_ref[core, :, :half] = y[:, at]
            half_ref[core, :, half:] = dx[:, at]
        core = lax.rem(lax.axis_index("seq"), 2)
        out_ref[...] = half_ref[1 - core]
        keep_ref[...] = half_ref[core]

    x_rows, dy_rows, act, dh, out, keep = call(
        expert_kernel,
        [((slots, width), BF16)] * 2
        + [((slots, hidden_part), BF16)] * 2
        + [((slots, width), F32)] * 2,
        EXPERT_MIB,
        8 * slots * width * hidden_part,
        4 * width * hidden_part,
        [
            pltpu.VMEM((2, slots, width), F32),
        ],
    )(w2, rows_in, w1)

    def pack_back_kernel(l_ref, r_ref, send_ref):
        full = l_ref[...] + r_ref[...]
        for c in range(ne):
            chunk = full[c * per : (c + 1) * per].astype(BF16)
            for s in range(ns):
                send_ref[s * ne + c] = chunk

    (send,) = call(
        pack_back_kernel,
        [((ns * ne, per, width), BF16)],
        PACK_MIB,
        2 * slots * width,
        8 * slots * width,
    )(keep, to_seq(out, 1))
    rows_back = to_all(send)

    def outer(steps, build, shapes, *operands):
        def body(*refs):
            ins, outs, done_ref, near, sems = refs[:-6], refs[-6:-4], refs[-4], refs[-3:-1], refs[-1]
            pairs = build(*[r[...] for r in ins])
            copies = []
            for n in range(steps):
                for m, (left, right) in enumerate(pairs):
                    step = near[m].shape[0] // steps
                    at = slice(n * step, (n + 1) * step)
                    near[m][at] = dot(left[:, at], right, 0, 0).astype(BF16)
                    copy = pltpu.make_async_copy(near[m].at[at], outs[m].at[at], sems.at[2 * n + m])
                    copy.start()
                    copies.append(copy)
            done_ref[...] = jnp.zeros((8, LANES), F32)
            for copy in copies:
                copy.wait()

        return call(
            body,
            [(shape, BF16) for shape in shapes] + [((8, LANES), F32)],
            16,
            OUTER_FLOPS,
            sum(2 * m * n for m, n in shapes),
            [pltpu.VMEM(shape, BF16) for shape in shapes] + [pltpu.SemaphoreType.DMA((2 * steps,))],
            out_hbm=(0, 1),
        )(*operands)

    d_w_out, d_w_in, written = outer(
        5,
        lambda act, dy, x, dh: ((act, dy), (x, dh)),
        ((hidden_part, width), (width, hidden_part)),
        act,
        dy_rows,
        x_rows,
        dh,
    )

    def merge_kernel(l_ref, r_ref, out_ref):
        a, *stats = merged(l_ref, r_ref)
        out_ref[:, :width] = a
        out_ref[:, width:] = stat_tile(*stats)

    bits = (ns - 1).bit_length()
    for bit in range(1, bits - 1):
        (part,) = call(
            merge_kernel, [((slots, wide), F32)], 8, 4 * slots * width, 12 * slots * width
        )(part, to_seq(part, 1 << bit))

    def softmax_kernel(_, l_ref, r_ref, route_ref, x_ref, row_ref, combine_ref, dispatch_ref):
        a, top, total, total_b = merged(l_ref, r_ref)
        row_ref[...] = a / total_b
        logits = dot(route_ref[...], x_ref[...], 1, 1)
        e = jnp.exp(logits - jnp.max(logits, axis=0, keepdims=True))
        combine_ref[...] = e / jnp.sum(e, axis=0, keepdims=True)
        dispatch_ref[...] = jnp.exp(logits - top) / total

    clip_rows, combine, dispatch = call(
        softmax_kernel,
        [((slots, width), F32), ((slots, length), F32), ((slots, length), F32)],
        8,
        2 * slots * length * width,
        2 * length * width,
        in_hbm=(0,),
    )(written, part, to_seq(part, 1 << (bits - 1)), router.T, feats)

    def logit_kernel(in_ref, a_ref, c_ref, d_ref, x_ref, g_ref, l_ref, y_ref, dx_ref, out):
        y, dx = [], []
        for core in range(2):
            got = [sum(in_ref[s * ne + e].astype(F32) for s in range(core, ns, 2)) for e in range(ne)]
            both = jnp.concatenate(got, axis=0)
            y.append(both[:, :half])
            dx.append(both[:, half:])
        y, dx = (jnp.concatenate(v, axis=1).astype(BF16) for v in (y, dx))
        dxf = dx.astype(F32)
        inner = jnp.sum(dxf * a_ref[...], axis=1, keepdims=True)
        x = x_ref[...]
        combine = c_ref[...]
        dispatch = d_ref[...]
        d_combine = dot(y, g_ref[...], 1, 1)
        d_c = combine * (d_combine - jnp.sum(combine * d_combine, axis=0, keepdims=True))
        d_d = dispatch * (dot(dx, x, 1, 1) - inner)
        d_logit = (d_c + d_d).astype(BF16)
        d_route = dot(d_logit, x, 1, 0).astype(BF16)
        l_ref[...] = d_logit
        y_ref[...] = y
        dx_ref[...] = dx
        for k in range(ns * ne):
            piece = d_route[:, k * cut : (k + 1) * cut]
            out[k] = jnp.concatenate([piece[: slots // 2], piece[slots // 2 :]], axis=1)

    d_logit, y, dx, send = call(
        logit_kernel,
        [
            ((slots, length), BF16),
            ((slots, width), BF16),
            ((slots, width), BF16),
            ((ns * ne, slots // 2, 2 * cut), BF16),
        ],
        24,
        6 * slots * length * width,
        4 * length * width,
    )(rows_back, clip_rows, combine, dispatch, feats, cotangent)
    chunks = to_all(send)

    def token_products(combine, dispatch, d_logit, y, dx, route):
        left = jnp.concatenate([dispatch, d_logit.astype(F32)], axis=0).astype(BF16)
        right = jnp.concatenate([dx.astype(F32), route.astype(F32)], axis=0).astype(BF16)
        return (combine.astype(BF16), y), (left, right)

    mixed, d_feats, _ = outer(
        4, token_products, ((length, width),) * 2, combine, dispatch, d_logit, y, dx, router.T
    )

    def sum_kernel(in_ref, out_ref):
        full = jnp.sum(in_ref[...].astype(F32), axis=0)
        out_ref[...] = jnp.concatenate([full[:, :cut], full[:, cut:]], axis=0)

    (d_router,) = call(
        sum_kernel, [((slots, cut), F32)], 8, slots * width, slots * width * 4
    )(chunks)
    return mixed[None], d_feats[None], d_router.T, d_w_in[None], d_w_out[None]


def solution(mesh):
    in_specs = (
        P("exp", "seq", None),
        P(),
        P("exp", None, "seq"),
        P("exp", "seq", None),
        P("exp", "seq", None),
    )
    out_specs = (
        P("exp", "seq", None),
        P("exp", "seq", None),
        P(("seq", "exp"), None),
        P("exp", None, "seq"),
        P("exp", "seq", None),
    )
    body = functools.partial(shards, mesh.shape["seq"], mesh.shape["exp"])
    return jax.shard_map(body, mesh=mesh, in_specs=in_specs, out_specs=out_specs, check_vma=False)
```

```python
import functools
import math

import jax
import jax.numpy as jnp
from jax import lax
from jax.experimental import pallas as pl
from jax.experimental.pallas import tpu as pltpu
from jax.sharding import PartitionSpec as P

F32 = jnp.float32
BF16 = jnp.bfloat16
LANES = 128
FIRST_FLOPS = 1 << 40
PACK_MIB = 8
EXPERT_MIB = 24
PACK_FLOPS = 1 << 36
OUTER_FLOPS = 1 << 36
VMEM = pl.BlockSpec(memory_space=pltpu.VMEM)
HBM = pl.BlockSpec(memory_space=pltpu.HBM)


def dot(a, b, ca, cb):
    return lax.dot_general(a, b, (((ca,), (cb,)), ((), ())), preferred_element_type=F32)


def pieces(x):
    hi = x.astype(BF16)
    rest = x - hi.astype(F32)
    mid = rest.astype(BF16)
    return hi, mid, (rest - mid.astype(F32)).astype(BF16)


ERFC = (
    0.17087277, -0.82215223, 1.48851587, -1.13520398, 0.27886807,
    -0.18628806, 0.09678418, 0.37409196, 1.00002368, -1.26551223,
)


def gelu_parts(h):
    z = jnp.abs(h) * math.sqrt(0.5)
    t = 1.0 / (1.0 + 0.5 * z)
    poly = jnp.full_like(t, ERFC[0])
    for coefficient in ERFC[1:]:
        poly = poly * t + coefficient
    tail = 0.5 * t * jnp.exp(poly - z * z)
    cdf = jnp.where(h < 0, tail, 1.0 - tail)
    pdf = jnp.exp(-0.5 * h * h) * (1.0 / math.sqrt(2.0 * math.pi))
    return h * cdf, cdf + h * pdf


def call(body, out, vmem_mib, flops, nbytes, scratch=(), in_hbm=(), out_hbm=()):
    def run(*args):
        specs = [HBM if n in in_hbm else VMEM for n in range(len(args))]
        return pl.pallas_call(
            body,
            out_shape=tuple(jax.ShapeDtypeStruct(s, d) for s, d in out),
            in_specs=specs,
            out_specs=tuple(HBM if n in out_hbm else VMEM for n in range(len(out))),
            scratch_shapes=list(scratch),
            compiler_params=pltpu.CompilerParams(vmem_limit_bytes=int(vmem_mib * 2**20)),
            cost_estimate=pl.CostEstimate(flops=flops, bytes_accessed=nbytes, transcendentals=0),
        )(*args)

    return run


def shards(ns, ne, tokens, router, w_in, w_out, grad_out):
    feats, cotangent, w1, w2 = tokens[0], grad_out[0], w_in[0], w_out[0]
    length, width = feats.shape
    slots = router.shape[1]
    per = slots // ne
    hidden_part = w1.shape[1]
    half = width // 2
    wide = width + LANES
    cut = width // (ns * ne)

    def to_seq(x, k):
        return lax.ppermute(x, "seq", [(i, i ^ k) for i in range(ns)])

    def to_all(x):
        return lax.all_to_all(x, ("seq", "exp"), 0, 0, tiled=True)

    def stat_tile(*columns):
        lane = lax.broadcasted_iota(jnp.int32, (slots, LANES), 1)
        tile = jnp.zeros((slots, LANES), F32)
        for n, v in enumerate(columns):
            tile = jnp.where(lane == n, v.astype(F32), tile)
        return tile

    def first_kernel(out_ref):
        out_ref[...] = jnp.zeros((8, LANES), F32)

    (begun,) = call(first_kernel, [((8, LANES), F32)], 8, FIRST_FLOPS, 0)()

    def token_kernel(x_ref, r_ref, _, part_ref, combine_ref):
        x = x_ref[...]
        logits = dot(r_ref[...], x, 1, 1)
        top = jnp.max(logits, axis=1, keepdims=True)
        p = jnp.exp(logits - top)
        p_b = p.astype(BF16)
        total = jnp.sum(p, axis=1, keepdims=True)
        total_b = jnp.sum(p_b.astype(F32), axis=1, keepdims=True)
        e = jnp.exp(logits - jnp.max(logits, axis=0, keepdims=True))
        combine_ref[...] = (e / jnp.sum(e, axis=0, keepdims=True)).astype(BF16)
        part_ref[:, :width] = dot(p_b, x, 1, 0)
        part_ref[:, width:] = stat_tile(top, total, total_b)

    part, combine_b = call(
        token_kernel,
        [((slots, wide), F32), ((slots, length), BF16)],
        24,
        4 * slots * length * width,
        2 * length * width,
        in_hbm=(2,),
    )(feats, router.T, begun)

    def cotangent_kernel(p_ref, c_ref, g_ref, part_ref, keep_ref, half_ref):
        part_ref[:, :wide] = p_ref[...]
        b = dot(c_ref[...], g_ref[...], 1, 0)
        half_ref[0] = b[:, :half]
        half_ref[1] = b[:, half:]
        core = lax.rem(lax.axis_index("seq"), 2)
        part_ref[:, wide:] = half_ref[1 - core]
        keep_ref[...] = half_ref[core]

    part, keep = call(
        cotangent_kernel,
        [((slots, wide + half), F32), ((slots, half), F32)],
        24,
        2 * slots * length * width,
        2 * length * width,
        [pltpu.VMEM((2, slots, half), F32)],
    )(part, combine_b, cotangent)

    def merged(l_ref, r_ref):
        tops, totals, totals_b = (
            [r[:, width + n : width + n + 1] for r in (l_ref, r_ref)] for n in range(3)
        )
        top = jnp.maximum(*tops)
        scale = [jnp.exp(m - top) for m in tops]
        total, total_b = (scale[0] * v[0] + scale[1] * v[1] for v in (totals, totals_b))
        return scale[0] * l_ref[:, :width] + scale[1] * r_ref[:, :width], top, total, total_b

    def pack_kernel(l_ref, r_ref, keep_ref, part_ref, send_ref, half_ref):
        a, top, total, total_b = merged(l_ref, r_ref)
        part_ref[:, :width] = a
        part_ref[:, width:] = stat_tile(top, total, total_b)
        half_ref[0] = a[:, :half]
        half_ref[1] = a[:, half:]
        a = half_ref[lax.rem(lax.axis_index("seq"), 2)]
        b = keep_ref[...] + r_ref[:, wide:]
        rows = jnp.concatenate([a, b, stat_tile(*pieces(top), *pieces(total_b))], axis=1)
        for e in range(ne):
            chunk = rows[e * per : (e + 1) * per].astype(BF16)
            for s in range(ns):
                send_ref[s * ne + e] = chunk

    part, send = call(
        pack_kernel,
        [((slots, wide), F32), ((ns * ne, per, wide), BF16)],
        PACK_MIB,
        PACK_FLOPS,
        8 * slots * wide,
        [pltpu.VMEM((2, slots, half), F32)],
    )(part, to_seq(part, 1), keep)
    rows_in = to_all(send)

    def expert_kernel(*refs):
        w2_ref, in_ref, w1_ref, x_ref, dy_ref, act_ref, dh_ref, out_ref, keep_ref, *scratch = refs
        (half_ref,) = scratch
        tops, totals = [], []
        for s in range(0, ns, 2):
            tile = jnp.concatenate(
                [in_ref[s * ne + c, :, width:].astype(F32) for c in range(ne)], axis=0
            )
            tops.append(tile[:, 0:1] + tile[:, 1:2] + tile[:, 2:3])
            totals.append(tile[:, 3:4] + tile[:, 4:5] + tile[:, 5:6])
        top = functools.reduce(jnp.maximum, tops)
        scale = [jnp.exp(m - top) for m in tops]
        total = sum(w * v for w, v in zip(scale, totals))
        scale = [w / total for w in scale]
        xs, dys = [[], []], [[], []]
        for core in range(2):
            for c in range(ne):
                at = slice(c * per, (c + 1) * per)
                x, dy = 0.0, 0.0
                for w, s in zip(scale, range(core, ns, 2)):
                    x += w[at] * in_ref[s * ne + c, :, :half].astype(F32)
                    dy += in_ref[s * ne + c, :, half:width].astype(F32)
                xs[core].append(x)
                dys[core].append(dy)
        x, dy = (
            jnp.concatenate([jnp.concatenate(v, axis=0) for v in side], axis=1).astype(BF16)
            for side in (xs, dys)
        )
        x_ref[...] = x
        dy_ref[...] = dy
        w2v = w2_ref[...]
        d_act = dot(dy, w2v, 1, 1)
        act, slope = gelu_parts(dot(x, w1_ref[...], 1, 0))
        act = act.astype(BF16)
        act_ref[...] = act
        dh = (d_act * slope).astype(BF16)
        dh_ref[...] = dh
        y = dot(act, w2v, 1, 0)
        dx = dot(dh, w1_ref[...], 1, 1)
        for core in range(2):
            at = slice(core * half, (core + 1) * half)
            half_ref[core, :, :half] = y[:, at]
            half_ref[core, :, half:] = dx[:, at]
        core = lax.rem(lax.axis_index("seq"), 2)
        out_ref[...] = half_ref[1 - core].astype(BF16)
        keep_ref[...] = half_ref[core]

    x_rows, dy_rows, act, dh, out, keep = call(
        expert_kernel,
        [((slots, width), BF16)] * 2
        + [((slots, hidden_part), BF16)] * 2
        + [((slots, width), BF16), ((slots, width), F32)],
        EXPERT_MIB,
        8 * slots * width * hidden_part,
        4 * width * hidden_part,
        [
            pltpu.VMEM((2, slots, width), F32),
        ],
    )(w2, rows_in, w1)

    def pack_back_kernel(l_ref, r_ref, send_ref):
        full = l_ref[...] + r_ref[...].astype(F32)
        for c in range(ne):
            chunk = full[c * per : (c + 1) * per].astype(BF16)
            for s in range(ns):
                send_ref[s * ne + c] = chunk

    (send,) = call(
        pack_back_kernel,
        [((ns * ne, per, width), BF16)],
        PACK_MIB,
        2 * slots * width,
        8 * slots * width,
    )(keep, to_seq(out, 1))
    rows_back = to_all(send)

    def outer(steps, build, shapes, *operands):
        def body(*refs):
            ins, outs, done_ref, near, sems = refs[:-6], refs[-6:-4], refs[-4], refs[-3:-1], refs[-1]
            pairs = build(*[r[...] for r in ins])
            copies = []
            for n in range(steps):
                for m, (left, right) in enumerate(pairs):
                    step = near[m].shape[0] // steps
                    at = slice(n * step, (n + 1) * step)
                    near[m][at] = dot(left[:, at], right, 0, 0).astype(BF16)
                    copy = pltpu.make_async_copy(near[m].at[at], outs[m].at[at], sems.at[2 * n + m])
                    copy.start()
                    copies.append(copy)
            done_ref[...] = jnp.zeros((8, LANES), F32)
            for copy in copies:
                copy.wait()

        return call(
            body,
            [(shape, BF16) for shape in shapes] + [((8, LANES), F32)],
            16,
            OUTER_FLOPS,
            sum(2 * m * n for m, n in shapes),
            [pltpu.VMEM(shape, BF16) for shape in shapes] + [pltpu.SemaphoreType.DMA((2 * steps,))],
            out_hbm=(0, 1),
        )(*operands)

    d_w_out, d_w_in, written = outer(
        5,
        lambda act, dy, x, dh: ((act, dy), (x, dh)),
        ((hidden_part, width), (width, hidden_part)),
        act,
        dy_rows,
        x_rows,
        dh,
    )

    def merge_kernel(l_ref, r_ref, out_ref):
        a, *stats = merged(l_ref, r_ref)
        out_ref[:, :width] = a
        out_ref[:, width:] = stat_tile(*stats)

    bits = (ns - 1).bit_length()
    for bit in range(1, bits - 1):
        (part,) = call(
            merge_kernel, [((slots, wide), F32)], 8, 4 * slots * width, 12 * slots * width
        )(part, to_seq(part, 1 << bit))

    def softmax_kernel(_, l_ref, r_ref, route_ref, x_ref, row_ref, combine_ref, dispatch_ref):
        a, top, total, total_b = merged(l_ref, r_ref)
        row_ref[...] = a / total_b
        logits = dot(route_ref[...], x_ref[...], 1, 1)
        e = jnp.exp(logits - jnp.max(logits, axis=0, keepdims=True))
        combine_ref[...] = e / jnp.sum(e, axis=0, keepdims=True)
        dispatch_ref[...] = jnp.exp(logits - top) / total

    clip_rows, combine, dispatch = call(
        softmax_kernel,
        [((slots, width), F32), ((slots, length), F32), ((slots, length), F32)],
        8,
        2 * slots * length * width,
        2 * length * width,
        in_hbm=(0,),
    )(written, part, to_seq(part, 1 << (bits - 1)), router.T, feats)

    def logit_kernel(in_ref, a_ref, c_ref, d_ref, x_ref, g_ref, l_ref, y_ref, dx_ref, out):
        y, dx = [], []
        for core in range(2):
            got = [sum(in_ref[s * ne + e].astype(F32) for s in range(core, ns, 2)) for e in range(ne)]
            both = jnp.concatenate(got, axis=0)
            y.append(both[:, :half])
            dx.append(both[:, half:])
        y, dx = (jnp.concatenate(v, axis=1).astype(BF16) for v in (y, dx))
        dxf = dx.astype(F32)
        inner = jnp.sum(dxf * a_ref[...], axis=1, keepdims=True)
        x = x_ref[...]
        combine = c_ref[...]
        dispatch = d_ref[...]
        d_combine = dot(y, g_ref[...], 1, 1)
        d_c = combine * (d_combine - jnp.sum(combine * d_combine, axis=0, keepdims=True))
        d_d = dispatch * (dot(dx, x, 1, 1) - inner)
        d_logit = (d_c + d_d).astype(BF16)
        d_route = dot(d_logit, x, 1, 0)
        l_ref[...] = d_logit
        y_ref[...] = y
        dx_ref[...] = dx
        for k in range(ns * ne):
            piece = d_route[:, k * cut : (k + 1) * cut]
            out[k] = jnp.concatenate([piece[: slots // 2], piece[slots // 2 :]], axis=1).astype(BF16)

    d_logit, y, dx, send = call(
        logit_kernel,
        [
            ((slots, length), BF16),
            ((slots, width), BF16),
            ((slots, width), BF16),
            ((ns * ne, slots // 2, 2 * cut), BF16),
        ],
        24,
        6 * slots * length * width,
        4 * length * width,
    )(rows_back, clip_rows, combine, dispatch, feats, cotangent)
    chunks = to_all(send)

    def token_products(combine, dispatch, d_logit, y, dx, route):
        left = jnp.concatenate([dispatch, d_logit.astype(F32)], axis=0).astype(BF16)
        right = jnp.concatenate([dx.astype(F32), route.astype(F32)], axis=0).astype(BF16)
        return (combine.astype(BF16), y), (left, right)

    mixed, d_feats, _ = outer(
        4, token_products, ((length, width),) * 2, combine, dispatch, d_logit, y, dx, router.T
    )

    def sum_kernel(in_ref, out_ref):
        full = jnp.sum(in_ref[...].astype(F32), axis=0)
        out_ref[...] = jnp.concatenate([full[:, :cut], full[:, cut:]], axis=0)

    (d_router,) = call(
        sum_kernel, [((slots, cut), F32)], 8, slots * width, slots * width * 4
    )(chunks)
    return mixed[None], d_feats[None], d_router.T, d_w_in[None], d_w_out[None]


def solution(mesh):
    in_specs = (
        P("exp", "seq", None),
        P(),
        P("exp", None, "seq"),
        P("exp", "seq", None),
        P("exp", "seq", None),
    )
    out_specs = (
        P("exp", "seq", None),
        P("exp", "seq", None),
        P(("seq", "exp"), None),
        P("exp", None, "seq"),
        P("exp", "seq", None),
    )
    body = functools.partial(shards, mesh.shape["seq"], mesh.shape["exp"])
    return jax.shard_map(body, mesh=mesh, in_specs=in_specs, out_specs=out_specs, check_vma=False)
```
